256 devices in a mesh: pitch: 32 (over y, z), span: 8 (over x, core).
Axes of the slice: x: 4, y: 4, z: 8, core: 2. Of those that a mesh axis runs over, the one named last changes fastest.
Arguments:
- fields: float32 [5, 256, 65536], P(None, 'span', 'pitch'), may hold values from -10 to 10
- diffusivity: float32 [256, 65536], P('span', 'pitch'), may hold values from 0.1 to 0.24
- mixing: float32 [256, 256], replicated, may hold values from -0.375 to 0.375
- cond_gain: float32 [5], replicated, may hold values from -1 to 1
- advection: float32 [5, 2], replicated, may hold values from -0.35 to 0.35
- parcels: float32 [16, 2097152], P(None, ('pitch', 'span')), may hold values from -6 to 6
- cell: int32 [2097152], P(('pitch', 'span')), may hold values from 0 to 65535
- couple: float32 [5, 16], replicated, may hold values from -1.5 to 1.5
- relax: float32 [16], replicated, may hold values from 0.02 to 0.9
- drag: float32 [16, 5], replicated, may hold values from -2.5 to 2.5
- counts: int32 [8192], P(('pitch', 'span')), may hold values from 0 to 512, as said below
Outputs:
- new_fields: float32 [5, 256, 65536], P(None, 'span', 'pitch')
- arrived: float32 [16, 4194304], P(None, ('pitch', 'span'))
The draws below stay inside these ranges and needn't reach their ends.
Inputs may be any that keep to these rules, and one draw needn't show every extreme that they name: `counts`: each device's entries sum to 8192; one pitch index, drawn from the seed, gets exactly 512 parcels from every device.
All inputs are finite; a program needn't handle non-finite values.
Results may differ from the reference program's by a relative error of at most 0.000086.
Values sent between devices are 32-bit elements; how exact they have to be, the bound alone decides.
A program may use at most 128 MiB of HBM per device.

```python
import math
import jax
import jax.numpy as jnp
from jax import lax

F = 5
Q = 16
SUBSTEPS = 2
CR = 32
CP = 2048
PD = 8192
NR = 256
NC = 65536
CAP = 512
NPAR = 2097152
N_PITCH = 32
N_SPAN = 8
DEVICES = 256


def draw_fields(key, part):
    first = jax.random.fold_in(key, 11)
    second = jax.random.fold_in(key, 12)
    means = jnp.clip(jax.random.normal(first, (F, NR, 1), jnp.float32), -3.0, 3.0)
    noise = jnp.clip(jax.random.normal(second, (F, NR, NC), jnp.float32), -5.0, 5.0)
    return (means + noise).astype(jnp.float32)


def draw_counts(key, part):
    others = N_PITCH - 1
    base = (PD - CAP) // others
    leftover = PD - CAP - base * others
    heavy = jax.random.randint(jax.random.fold_in(key, 1), (), 0, N_PITCH)
    pairs = others // 2
    jitter = jax.random.randint(jax.random.fold_in(key, 2), (DEVICES, pairs), 0, base // 4 + 1)
    signed = jnp.stack([jitter, -jitter], axis=2).reshape(DEVICES, 2 * pairs)
    if others % 2 == 1:
        signed = jnp.concatenate([signed, jnp.zeros((DEVICES, 1), jnp.int32)], axis=1)
    position = jnp.arange(others, dtype=jnp.int32)
    values = base + signed + (position < leftover).astype(jnp.int32)[None, :]
    offset = jax.random.randint(jax.random.fold_in(key, 3), (DEVICES, 1), 0, others)
    target = (heavy + 1 + (position[None, :] + offset) % others) % N_PITCH
    owners = jnp.broadcast_to(jnp.arange(DEVICES, dtype=jnp.int32)[:, None], target.shape)
    table = jnp.zeros((DEVICES, N_PITCH), jnp.int32).at[owners, target].set(values)
    table = table.at[:, heavy].set(CAP)
    return table.reshape(-1).astype(jnp.int32)


def set_ends(entries, key, least, top_value):
    extent = entries.shape
    spot = [jax.random.randint(jax.random.fold_in(key, axis), (), 0, extent[axis]) for axis in range(len(extent))]
    entries = entries.at[tuple(spot)].set(least)
    longest = extent.index(max(extent))
    spot[longest] = (spot[longest] + 1) % extent[longest]
    return entries.at[tuple(spot)].set(top_value)


def shard_levels(stream_key, shape, pieces, low, top_value):
    def one(axis_at, blocks):
        draws = jax.random.uniform(jax.random.fold_in(jax.random.fold_in(stream_key, 6), axis_at), (blocks,), jnp.float32, low / len(pieces), top_value / len(pieces))
        return jnp.repeat(jnp.exp(draws), shape[axis_at] // blocks).reshape((-1,) + (1,) * (len(shape) - axis_at - 1))

    gain = one(*pieces[0])
    for cut in pieces[1:]:
        gain = gain * one(*cut)
    return gain


def scatter_about(stream_key, extent, deviation, reach, split=(), held_as=jnp.bfloat16):
    values = deviation * jax.random.normal(stream_key, extent, jnp.float32)
    if split:
        values = values * shard_levels(stream_key, extent, split, -0.22, 0.18)
    return jnp.clip(values, -reach, reach).astype(held_as)


def setup_inputs(seed: int = 0) -> dict:
    keys = jax.random.split(jax.random.key(seed), 12)
    return {
        "fields": draw_fields(jax.random.fold_in(keys[11], 71), 0),
        "diffusivity": jnp.clip(jnp.exp(math.log(0.24) - 0.8754687 * jax.random.uniform(keys[1], (NR, NC), jnp.float32) ** shard_levels(keys[1], (NR, NC), ((0, 8), (1, 32)), -0.2, 0.2)), 0.1, 0.24),
        "mixing": scatter_about(keys[2], (NR, NR), NR ** -0.5, 0.375, (), jnp.float32),
        "cond_gain": jnp.clip(jax.random.uniform(keys[3], (F,), jnp.float32, -1.0, 1.0), -1.0, 1.0),
        "advection": jnp.clip(jax.random.uniform(keys[4], (F, 2), jnp.float32, -0.35, 0.35), -0.35, 0.35),
        "parcels": scatter_about(keys[5], (Q, NPAR), 1.0, 6.0, ((1, 256),), jnp.float32),
        "cell": set_ends(jax.random.randint(keys[6], (NPAR,), 0, CR * CP), jax.random.fold_in(keys[6], 1), 0, (CR * CP) - 1).astype(jnp.int32),
        "couple": scatter_about(keys[7], (F, Q), Q ** -0.5, 1.5, (), jnp.float32),
        "relax": jnp.clip(jnp.exp(jax.random.uniform(keys[8], (Q,), jnp.float32, math.log(0.02), math.log(0.9))), 0.02, 0.9),
        "drag": scatter_about(keys[9], (Q, F), F ** -0.5, 2.5, (), jnp.float32),
        "counts": draw_counts(jax.random.fold_in(keys[11], 71), 0),
    }


def advance(padded, source, nu, advection):
    centre = padded[:, 1:-1, 1:-1]
    upper = padded[:, 2:, 1:-1]
    lower = padded[:, :-2, 1:-1]
    right = padded[:, 1:-1, 2:]
    left_side = padded[:, 1:-1, :-2]
    radial = advection[:, 0][:, None, None]
    across = advection[:, 1][:, None, None]
    return (centre + 0.25 * source + radial * (upper - lower) + across * (right - left_side)
            + nu * (upper + lower + right + left_side - 4.0 * centre))


def reference(fields, diffusivity, mixing, cond_gain, advection, parcels, cell, couple, relax, drag, counts):
    high = lax.Precision.HIGHEST
    total = PD * DEVICES
    device = jnp.arange(total, dtype=jnp.int32) // PD
    pitch_of = device // N_SPAN
    span_of = device % N_SPAN
    rowidx = span_of * CR + cell // CP
    colidx = pitch_of * CP + cell % CP
    flat = rowidx * NC + colidx
    proj = jnp.dot(couple, parcels, precision=high, preferred_element_type=jnp.float32)
    deposit = jnp.zeros((F, NR * NC), jnp.float32).at[:, flat].add(proj).reshape(F, NR, N_PITCH, CP)
    blocks = fields.reshape(F, NR, N_PITCH, CP)
    profile = jnp.mean(blocks, axis=3)
    corr = jnp.einsum("rs,fsb->frb", mixing, profile, precision=high)
    rate = jax.nn.softplus(blocks[0] + corr[0][:, :, None]) * (1.0 + jnp.tanh(blocks[1] + corr[1][:, :, None]))
    source = cond_gain[:, None, None, None] * rate[None] - 0.5 * corr[:, :, :, None] + deposit
    source = source.reshape(F, NR, NC)
    state = fields
    for step in range(SUBSTEPS):
        padded = jnp.pad(state, ((0, 0), (1, 1), (1, 1)))
        state = advance(padded, source, diffusivity[None], advection)
    local_fluid = fields.reshape(F, NR * NC)[:, flat]
    moved = (1.0 - relax[:, None]) * parcels + jnp.dot(drag, local_fluid, precision=high, preferred_element_type=jnp.float32)
    table = counts.reshape(DEVICES, N_PITCH)
    offsets = jnp.cumsum(table, axis=1).astype(jnp.int32) - table
    dest_p = jnp.arange(N_PITCH, dtype=jnp.int32)[:, None, None, None]
    span_s = jnp.arange(N_SPAN, dtype=jnp.int32)[None, :, None, None]
    source_p = jnp.arange(N_PITCH, dtype=jnp.int32)[None, None, :, None]
    slot = jnp.arange(CAP, dtype=jnp.int32)[None, None, None, :]
    sender = source_p * N_SPAN + span_s
    live = table[sender, dest_p]
    start = offsets[sender, dest_p]
    valid = slot < live
    index = jnp.where(valid, sender * PD + start + slot, 0).reshape(-1)
    arrived = jnp.where(valid.reshape(-1)[None, :], moved[:, index], 0.0)
    return state, arrived
```

```python
import functools

import jax
import jax.numpy as jnp
from jax import lax
from jax.experimental import pallas as pl
from jax.experimental.pallas import tpu as pltpu
from jax.sharding import PartitionSpec as P

F32, BF = jnp.float32, jnp.bfloat16
MESH = pl.DeviceIdType.MESH
A, B, KB = 128, 512, 512


def step_kernel(
    n_pitch,
    n_span,
    cap,
    counts,
    cond_gain,
    advection,
    cell,
    fields,
    nu,
    mixing,
    parcels,
    couple,
    relax,
    drag,
    new_fields,
    arrived,
    offs,
    table,
    total,
    moved,
    records,
    outgoing,
    profile,
    source,
    state,
    row_out,
    row_in,
    col_out,
    col_in,
    send_sem,
    recv_sem,
    prof_send,
    prof_recv,
    halo_send,
    halo_recv,
    own_sem,
):
    nf, rows, cols = fields.shape
    nq, npar = parcels.shape
    chunks = cols // B
    blocks = npar // KB
    me, sp = lax.axis_index("pitch"), lax.axis_index("span")
    pitch_next, pitch_prev = lax.rem(me + 1, n_pitch), lax.rem(me + n_pitch - 1, n_pitch)
    span_next, span_prev = lax.rem(sp + 1, n_span), lax.rem(sp + n_span - 1, n_span)

    barrier = pltpu.get_barrier_semaphore()

    def greet_pitch(k, _):
        pl.semaphore_signal(
            barrier, inc=1, device_id=(lax.rem(me + k, n_pitch), sp), device_id_type=MESH
        )
        return 0

    def greet_span(k, _):
        pl.semaphore_signal(
            barrier, inc=1, device_id=(me, lax.rem(sp + k, n_span)), device_id_type=MESH
        )
        return 0

    lax.fori_loop(1, n_pitch, greet_pitch, 0)
    lax.fori_loop(1, n_span, greet_span, 0)

    running = jnp.int32(0)
    for p in range(n_pitch):
        offs[p] = running
        running = running + counts[p]
    first = offs[pitch_next] // KB
    for s in range(blocks):
        records[s] = parcels[:, s * KB : (s + 1) * KB]

    for f in range(nf):
        for q in range(chunks):
            x = fields[f, :, q * B : (q + 1) * B]
            hi = x.astype(BF)
            at = f * A + q * rows
            table[at : at + rows, 0:B] = hi
            table[at : at + rows, B : 2 * B] = (x - hi.astype(F32)).astype(BF)

    lane = lax.broadcasted_iota(jnp.int32, (rows, 128), 1)
    mean = jnp.zeros((rows, 128), F32)
    left = jnp.zeros((rows, 128), F32)
    right = jnp.zeros((rows, 128), F32)
    for f in range(nf):
        x = fields[f]
        mean = jnp.where(lane == f, jnp.sum(x, axis=1, keepdims=True) * (1.0 / cols), mean)
        left = jnp.where(lane == f, x[:, 0:1], left)
        right = jnp.where(lane == f, x[:, cols - 1 : cols], right)
        row_out[0, f : f + 1, :] = x[0:1, :]
        row_out[1, f : f + 1, :] = x[rows - 1 : rows, :]
    col_out[0] = left
    col_out[1] = right
    mine = pl.ds(pl.multiple_of(sp * rows, rows), rows)
    profile[mine, :] = mean

    diag = lax.broadcasted_iota(jnp.int32, (nq, nq), 0) == lax.broadcasted_iota(
        jnp.int32, (nq, nq), 1
    )

    def column(line):
        return jnp.sum(jnp.where(diag, line, 0.0), axis=1, keepdims=True)

    keep = column(1.0 - relax[...])
    pull = [column(drag[f : f + 1, :]) for f in range(nf)]
    cp = couple[...]
    index_a = lax.broadcasted_iota(jnp.int32, (A, KB), 0)
    index_b = lax.broadcasted_iota(jnp.int32, (B, KB), 0)
    lane_q = lax.broadcasted_iota(jnp.int32, (nq, 128), 1)

    def block_of(s):
        return lax.rem(first + s, blocks)

    def cells_of(block):
        homes = cell[block]
        c = jnp.concatenate([homes[q : q + 1] for q in range(KB // 128)], axis=1)
        in_row = c & (cols - 1)
        hot_a = index_a == (in_row // B) * rows + c // cols
        hot_b = jnp.where(index_b == (in_row & (B - 1)), 1.0, 0.0).astype(BF)
        return hot_a, hot_b

    def gather(s):
        block = block_of(s)
        hot_a, hot_b = cells_of(block)
        picked = jnp.dot(
            table[...], jnp.concatenate([hot_b, hot_b], axis=0), preferred_element_type=F32
        )
        value = keep * records[block]
        for f in range(nf):
            fluid = jnp.sum(
                jnp.where(hot_a, picked[f * A : (f + 1) * A], 0.0), axis=0, keepdims=True
            )
            value = value + pull[f] * fluid
        for q in range(KB // 128):
            moved[s * (KB // 128) + q] = value[:, q * 128 : (q + 1) * 128]

    def pack(k, slot):
        p = lax.rem(me + k, n_pitch)
        count = counts[p]
        start = lax.rem(offs[p] - first * KB + npar, npar)
        tile = start // 128
        pieces = [moved[tile + q] for q in range(cap // 128 + 1)]
        shift = jnp.full((nq, 128), lax.rem(start, 128), jnp.int32)
        for bit in range(7):
            by = 1 << bit
            turned = [pltpu.roll(piece, 128 - by, axis=1) for piece in pieces]
            turned.append(turned[-1])
            pieces = [
                jnp.where(
                    (shift & by) != 0,
                    jnp.where(lane_q < 128 - by, turned[q], turned[q + 1]),
                    pieces[q],
                )
                for q in range(len(pieces))
            ]
        for q in range(cap // 128):
            outgoing[slot, :, q * 128 : (q + 1) * 128] = jnp.where(
                lane_q + q * 128 < count, pieces[q], 0.0
            )

    own_slots = pl.ds(pl.multiple_of(me * cap, cap), cap)

    def parcel_copy(k):
        return pltpu.make_async_remote_copy(
            src_ref=outgoing.at[k],
            dst_ref=arrived.at[:, own_slots],
            send_sem=send_sem.at[k],
            recv_sem=recv_sem.at[k],
            device_id=(lax.rem(me + k, n_pitch), sp),
            device_id_type=MESH,
        )

    def profile_copy(k):
        return pltpu.make_async_remote_copy(
            src_ref=profile.at[mine],
            dst_ref=profile.at[mine],
            send_sem=prof_send.at[k],
            recv_sem=prof_recv.at[k],
            device_id=(me, lax.rem(sp + k, n_span)),
            device_id_type=MESH,
        )

    def halo_copies(turn):
        copies = []
        for side in range(2):
            for kind, (out, into, target) in enumerate(
                (
                    (row_out, row_in, (me, (span_prev, span_next)[side])),
                    (col_out, col_in, ((pitch_prev, pitch_next)[side], sp)),
                )
            ):
                copies.append(
                    pltpu.make_async_remote_copy(
                        src_ref=out.at[2 * turn + side],
                        dst_ref=into.at[2 * turn + side],
                        send_sem=halo_send.at[4 * turn + 2 * side + kind],
                        recv_sem=halo_recv.at[4 * turn + 2 * side + kind],
                        device_id=target,
                        device_id_type=MESH,
                    )
                )
        return copies

    gather(0)
    for q in range(KB // 128):
        moved[npar // 128 + q] = moved[q]
    pl.semaphore_wait(barrier, n_pitch + n_span - 2)

    def start_profile(k, _):
        profile_copy(k).start()
        return 0

    lax.fori_loop(1, n_span, start_profile, 0)
    first_halo = halo_copies(0)
    for copy in first_halo:
        copy.start()

    def gather_and_send(s, _):
        gather(s)
        pack(s, s)
        parcel_copy(s).start()
        return 0

    lax.fori_loop(1, blocks, gather_and_send, 0)

    def send(k, _):
        pack(k, k)
        parcel_copy(k).start()
        return 0

    lax.fori_loop(blocks, n_pitch, send, 0)
    pack(n_pitch, 0)
    own_copy = pltpu.make_async_copy(outgoing.at[0], arrived.at[:, own_slots], own_sem)
    own_copy.start()

    total[...] = jnp.zeros_like(total)

    def scatter(s, _):
        hot_a, hot_b = cells_of(s)
        par = records[s]
        given = jnp.zeros((nf, KB), F32)
        for q in range(nq):
            given = given + cp[:, q : q + 1] * par[q : q + 1, :]
        hi = given.astype(BF).astype(F32)
        lo = given - hi
        spread = jnp.concatenate(
            [
                jnp.concatenate(
                    [jnp.where(hot_a, x[f : f + 1], 0.0).astype(BF) for f in range(nf)], axis=0
                )
                for x in (hi, lo)
            ],
            axis=1,
        )
        total[...] += lax.dot_general(
            spread,
            jnp.concatenate([hot_b, hot_b], axis=1),
            (((1,), (1,)), ((), ())),
            preferred_element_type=F32,
        )
        return 0

    lax.fori_loop(0, blocks, scatter, 0)

    def wait_profile(k, _):
        profile_copy(k).wait()
        return 0

    lax.fori_loop(1, n_span, wait_profile, 0)
    corr = jnp.dot(
        mixing[mine, :], profile[...], precision=lax.Precision.HIGHEST, preferred_element_type=F32
    )
    x = fields[0] + corr[:, 0:1]
    rate = (jnp.maximum(x, 0.0) + jnp.log1p(jnp.exp(-jnp.abs(x)))) * (
        1.0 + jnp.tanh(fields[1] + corr[:, 1:2])
    )
    source[0] = rate
    for f in reversed(range(nf)):
        deposit = jnp.concatenate(
            [total[f * A + q * rows : f * A + (q + 1) * rows, :] for q in range(chunks)], axis=1
        )
        source[f] = 0.25 * (cond_gain[f] * rate - 0.5 * corr[:, f : f + 1] + deposit)

    row_id = lax.broadcasted_iota(jnp.int32, (rows, cols), 0)
    col_id = lax.broadcasted_iota(jnp.int32, (rows, cols), 1)
    row_low = jnp.where(sp == 0, 0.0, 1.0)
    row_high = jnp.where(sp == n_span - 1, 0.0, 1.0)
    col_low = jnp.where(me == 0, 0.0, 1.0)
    col_high = jnp.where(me == n_pitch - 1, 0.0, 1.0)

    def advance(u, f, turn):
        below = row_in[2 * turn + 1, f : f + 1, :] * row_low
        above = row_in[2 * turn, f : f + 1, :] * row_high
        before = col_in[2 * turn + 1][:, f : f + 1] * col_low
        after = col_in[2 * turn][:, f : f + 1] * col_high
        upper = jnp.where(row_id == rows - 1, above, pltpu.roll(u, rows - 1, axis=0))
        lower = jnp.where(row_id == 0, below, pltpu.roll(u, 1, axis=0))
        ahead = jnp.where(col_id == cols - 1, after, pltpu.roll(u, cols - 1, axis=1))
        behind = jnp.where(col_id == 0, before, pltpu.roll(u, 1, axis=1))
        return (
            u
            + source[f]
            + advection[0, f] * (upper - lower)
            + advection[1, f] * (ahead - behind)
            + nu[...] * (upper + lower + ahead + behind - 4.0 * u)
        )

    for copy in first_halo:
        copy.wait()
    left = jnp.zeros((rows, 128), F32)
    right = jnp.zeros((rows, 128), F32)
    for f in range(nf):
        u = advance(fields[f], f, 0)
        state[f] = u
        left = jnp.where(lane == f, u[:, 0:1], left)
        right = jnp.where(lane == f, u[:, cols - 1 : cols], right)
        row_out[2, f : f + 1, :] = u[0:1, :]
        row_out[3, f : f + 1, :] = u[rows - 1 : rows, :]
    col_out[2] = left
    col_out[3] = right
    second_halo = halo_copies(1)
    for copy in second_halo:
        copy.start()
    for copy in second_halo:
        copy.wait()
    for f in range(nf):
        new_fields[f] = advance(state[f], f, 1)

    own_copy.wait()

    def wait_parcels(k, _):
        parcel_copy(k).wait()
        return 0

    lax.fori_loop(1, n_pitch, wait_parcels, 0)


def local(
    fields, diffusivity, mixing, cond_gain, advection, parcels, cell, couple, relax, drag, counts
):
    nf, rows, cols = fields.shape
    nq, npar = parcels.shape
    n_pitch, n_span = lax.axis_size("pitch"), lax.axis_size("span")
    cap = 2 * npar // n_pitch
    vmem = pl.BlockSpec(memory_space=pltpu.VMEM)
    smem = pl.BlockSpec(memory_space=pltpu.SMEM)
    dma = pltpu.SemaphoreType.DMA
    return pl.pallas_call(
        functools.partial(step_kernel, n_pitch, n_span, cap),
        out_shape=(
            jax.ShapeDtypeStruct(fields.shape, F32),
            jax.ShapeDtypeStruct((nq, n_pitch * cap), F32),
        ),
        in_specs=[smem] * 3 + [vmem] * 8,
        out_specs=(vmem, pl.BlockSpec(memory_space=pl.ANY)),
        scratch_shapes=[
            pltpu.SMEM((n_pitch,), jnp.int32),
            pltpu.VMEM((nf * A, 2 * B), BF),
            pltpu.VMEM((nf * A, B), F32),
            pltpu.VMEM(((npar + KB) // 128, nq, 128), F32),
            pltpu.VMEM((npar // KB, nq, KB), F32),
            pltpu.VMEM((n_pitch, nq, cap), F32),
            pltpu.VMEM((n_span * rows, 128), F32),
            pltpu.VMEM(fields.shape, F32),
            pltpu.VMEM(fields.shape, F32),
            pltpu.VMEM((4, 8, cols), F32),
            pltpu.VMEM((4, 8, cols), F32),
            pltpu.VMEM((4, rows, 128), F32),
            pltpu.VMEM((4, rows, 128), F32),
            dma((n_pitch,)),
            dma((n_pitch,)),
            dma((n_span,)),
            dma((n_span,)),
            dma((8,)),
            dma((8,)),
            dma,
        ],
        compiler_params=pltpu.CompilerParams(
            collective_id=0, has_side_effects=True, vmem_limit_bytes=48 << 20
        ),
        cost_estimate=pl.CostEstimate(
            flops=8 * nf * rows * cols * npar, bytes_accessed=6 << 20, transcendentals=0
        ),
    )(
        counts,
        cond_gain,
        advection.T,
        cell.reshape(npar // KB, KB // 128, 128),
        fields,
        diffusivity,
        mixing,
        parcels,
        couple,
        relax.reshape(1, nq),
        drag.T,
    )


def solution(mesh):
    return jax.shard_map(
        local,
        mesh=mesh,
        in_specs=(
            P(None, "span", "pitch"),
            P("span", "pitch"),
            P(),
            P(),
            P(),
            P(None, ("pitch", "span")),
            P(("pitch", "span")),
            P(),
            P(),
            P(),
            P(("pitch", "span")),
        ),
        out_specs=(P(None, "span", "pitch"), P(None, ("pitch", "span"))),
        check_vma=False,
    )
```

```python
import functools

import jax
import jax.numpy as jnp
from jax import lax
from jax.experimental import pallas as pl
from jax.experimental.pallas import tpu as pltpu
from jax.sharding import PartitionSpec as P

F32, BF = jnp.float32, jnp.bfloat16
MESH = pl.DeviceIdType.MESH
A, B, KB = 128, 512, 512


def step_kernel(
    n_pitch,
    n_span,
    cap,
    counts_hbm,
    gain_hbm,
    advection_hbm,
    cell_hbm,
    fields_hbm,
    nu_hbm,
    mixing_hbm,
    parcels_hbm,
    couple_hbm,
    relax_hbm,
    drag_hbm,
    new_fields,
    arrived,
    counts,
    cond_gain,
    advection,
    cell,
    fields,
    nu,
    mixing,
    couple,
    relax,
    drag,
    load_sem,
    record_sem,
    offs,
    table,
    total,
    moved,
    records,
    outgoing,
    profile,
    source,
    state,
    row_out,
    row_in,
    col_out,
    col_in,
    send_sem,
    recv_sem,
    prof_send,
    prof_recv,
    halo_send,
    halo_recv,
    own_sem,
):
    nf, rows, cols = fields.shape
    nq, npar = parcels_hbm.shape
    chunks = cols // B
    blocks = npar // KB
    me, sp = lax.axis_index("pitch"), lax.axis_index("span")
    pitch_next, pitch_prev = lax.rem(me + 1, n_pitch), lax.rem(me + n_pitch - 1, n_pitch)
    span_next, span_prev = lax.rem(sp + 1, n_span), lax.rem(sp + n_span - 1, n_span)

    loads = {}
    for n, (name, there, here) in enumerate(
        (
            ("counts", counts_hbm, counts),
            ("fields", fields_hbm, fields),
            ("cell", cell_hbm, cell),
            ("relax", relax_hbm, relax),
            ("drag", drag_hbm, drag),
            ("couple", couple_hbm, couple),
            ("mixing", mixing_hbm, mixing),
            ("nu", nu_hbm, nu),
            ("gain", gain_hbm, cond_gain),
            ("advection", advection_hbm, advection),
        )
    ):
        loads[name] = pltpu.make_async_copy(there, here, load_sem.at[n])
    for name in ("counts", "fields", "cell", "relax", "drag"):
        loads[name].start()
    record_loads = [
        pltpu.make_async_copy(
            parcels_hbm.at[:, s * KB : (s + 1) * KB], records.at[s], record_sem.at[s]
        )
        for s in range(blocks)
    ]
    for load in record_loads:
        load.start()
    for name in ("couple", "mixing", "nu", "gain", "advection"):
        loads[name].start()

    barrier = pltpu.get_barrier_semaphore()

    def greet_pitch(k, _):
        pl.semaphore_signal(
            barrier, inc=1, device_id=(lax.rem(me + k, n_pitch), sp), device_id_type=MESH
        )
        return 0

    def greet_span(k, _):
        pl.semaphore_signal(
            barrier, inc=1, device_id=(me, lax.rem(sp + k, n_span)), device_id_type=MESH
        )
        return 0

    lax.fori_loop(1, n_pitch, greet_pitch, 0)
    lax.fori_loop(1, n_span, greet_span, 0)

    loads["counts"].wait()
    running = jnp.int32(0)
    for p in range(n_pitch):
        offs[p] = running
        running = running + counts[p]
    first = offs[pitch_next] // KB
    loads["fields"].wait()

    for f in range(nf):
        for q in range(chunks):
            x = fields[f, :, q * B : (q + 1) * B]
            hi = x.astype(BF)
            at = f * A + q * rows
            table[at : at + rows, 0:B] = hi
            table[at : at + rows, B : 2 * B] = (x - hi.astype(F32)).astype(BF)

    lane = lax.broadcasted_iota(jnp.int32, (rows, 128), 1)
    mean = jnp.zeros((rows, 128), F32)
    left = jnp.zeros((rows, 128), F32)
    right = jnp.zeros((rows, 128), F32)
    for f in range(nf):
        x = fields[f]
        mean = jnp.where(lane == f, jnp.sum(x, axis=1, keepdims=True) * (1.0 / cols), mean)
        left = jnp.where(lane == f, x[:, 0:1], left)
        right = jnp.where(lane == f, x[:, cols - 1 : cols], right)
        row_out[0, f : f + 1, :] = x[0:1, :]
        row_out[1, f : f + 1, :] = x[rows - 1 : rows, :]
    col_out[0] = left
    col_out[1] = right
    mine = pl.ds(pl.multiple_of(sp * rows, rows), rows)
    profile[mine, :] = mean

    diag = lax.broadcasted_iota(jnp.int32, (nq, nq), 0) == lax.broadcasted_iota(
        jnp.int32, (nq, nq), 1
    )

    def column(line):
        return jnp.sum(jnp.where(diag, line, 0.0), axis=1, keepdims=True)

    for name in ("cell", "relax", "drag", "couple"):
        loads[name].wait()
    keep = column(1.0 - relax[...])
    pull = [column(drag[f : f + 1, :]) for f in range(nf)]
    cp = couple[...]
    index_a = lax.broadcasted_iota(jnp.int32, (A, KB), 0)
    index_b = lax.broadcasted_iota(jnp.int32, (B, KB), 0)
    lane_q = lax.broadcasted_iota(jnp.int32, (nq, 128), 1)

    def block_of(s):
        return lax.rem(first + s, blocks)

    def cells_of(block):
        homes = cell[block]
        c = jnp.concatenate([homes[q : q + 1] for q in range(KB // 128)], axis=1)
        in_row = c & (cols - 1)
        hot_a = index_a == (in_row // B) * rows + c // cols
        hot_b = jnp.where(index_b == (in_row & (B - 1)), 1.0, 0.0).astype(BF)
        return hot_a, hot_b

    def gather(s):
        block = block_of(s)
        hot_a, hot_b = cells_of(block)
        picked = jnp.dot(
            table[...], jnp.concatenate([hot_b, hot_b], axis=0), preferred_element_type=F32
        )
        value = keep * records[block]
        for f in range(nf):
            fluid = jnp.sum(
                jnp.where(hot_a, picked[f * A : (f + 1) * A], 0.0), axis=0, keepdims=True
            )
            value = value + pull[f] * fluid
        for q in range(KB // 128):
            moved[s * (KB // 128) + q] = value[:, q * 128 : (q + 1) * 128]

    def pack(k, slot):
        p = lax.rem(me + k, n_pitch)
        count = counts[p]
        start = lax.rem(offs[p] - first * KB + npar, npar)
        tile = start // 128
        pieces = [moved[tile + q] for q in range(cap // 128 + 1)]
        shift = lax.rem(start, 128)
        turned = [pltpu.roll(piece, lax.rem(128 - shift, 128), axis=1) for piece in pieces]
        for q in range(cap // 128):
            piece = jnp.where(lane_q < 128 - shift, turned[q], turned[q + 1])
            outgoing[slot, :, q * 128 : (q + 1) * 128] = jnp.where(
                lane_q + q * 128 < count, piece, 0.0
            )

    own_slots = pl.ds(pl.multiple_of(me * cap, cap), cap)

    def parcel_copy(k):
        return pltpu.make_async_remote_copy(
            src_ref=outgoing.at[k],
            dst_ref=arrived.at[:, own_slots],
            send_sem=send_sem.at[k],
            recv_sem=recv_sem.at[k],
            device_id=(lax.rem(me + k, n_pitch), sp),
            device_id_type=MESH,
        )

    def profile_copy(k):
        return pltpu.make_async_remote_copy(
            src_ref=profile.at[mine],
            dst_ref=profile.at[mine],
            send_sem=prof_send.at[k],
            recv_sem=prof_recv.at[k],
            device_id=(me, lax.rem(sp + k, n_span)),
            device_id_type=MESH,
        )

    def halo_copies(turn):
        copies = []
        for side in range(2):
            for kind, (out, into, target) in enumerate(
                (
                    (row_out, row_in, (me, (span_prev, span_next)[side])),
                    (col_out, col_in, ((pitch_prev, pitch_next)[side], sp)),
                )
            ):
                copies.append(
                    pltpu.make_async_remote_copy(
                        src_ref=out.at[2 * turn + side],
                        dst_ref=into.at[2 * turn + side],
                        send_sem=halo_send.at[4 * turn + 2 * side + kind],
                        recv_sem=halo_recv.at[4 * turn + 2 * side + kind],
                        device_id=target,
                        device_id_type=MESH,
                    )
                )
        return copies

    for load in record_loads:
        load.wait()
    gather(0)
    for q in range(KB // 128):
        moved[npar // 128 + q] = moved[q]
    pl.semaphore_wait(barrier, n_pitch + n_span - 2)

    def start_profile(k, _):
        profile_copy(k).start()
        return 0

    lax.fori_loop(1, n_span, start_profile, 0)
    first_halo = halo_copies(0)
    for copy in first_halo:
        copy.start()

    def gather_and_send(s, _):
        gather(s)
        pack(s, s)
        parcel_copy(s).start()
        return 0

    lax.fori_loop(1, blocks, gather_and_send, 0)

    def send(k, _):
        pack(k, k)
        parcel_copy(k).start()
        return 0

    lax.fori_loop(blocks, n_pitch, send, 0)
    pack(n_pitch, 0)
    own_copy = pltpu.make_async_copy(outgoing.at[0], arrived.at[:, own_slots], own_sem)
    own_copy.start()

    total[...] = jnp.zeros_like(total)

    def scatter(s, _):
        hot_a, hot_b = cells_of(s)
        par = records[s]
        given = jnp.zeros((nf, KB), F32)
        for q in range(nq):
            given = given + cp[:, q : q + 1] * par[q : q + 1, :]
        hi = given.astype(BF).astype(F32)
        lo = given - hi
        spread = jnp.concatenate(
            [
                jnp.concatenate(
                    [jnp.where(hot_a, x[f : f + 1], 0.0).astype(BF) for f in range(nf)], axis=0
                )
                for x in (hi, lo)
            ],
            axis=1,
        )
        total[...] += lax.dot_general(
            spread,
            jnp.concatenate([hot_b, hot_b], axis=1),
            (((1,), (1,)), ((), ())),
            preferred_element_type=F32,
        )
        return 0

    lax.fori_loop(0, blocks, scatter, 0)

    def wait_profile(k, _):
        profile_copy(k).wait()
        return 0

    lax.fori_loop(1, n_span, wait_profile, 0)
    for name in ("mixing", "nu", "gain", "advection"):
        loads[name].wait()
    corr = jnp.dot(
        mixing[mine, :], profile[...], precision=lax.Precision.HIGHEST, preferred_element_type=F32
    )
    x = fields[0] + corr[:, 0:1]
    rate = (jnp.maximum(x, 0.0) + jnp.log1p(jnp.exp(-jnp.abs(x)))) * (
        1.0 + jnp.tanh(fields[1] + corr[:, 1:2])
    )
    source[0] = rate
    for f in reversed(range(nf)):
        deposit = jnp.concatenate(
            [total[f * A + q * rows : f * A + (q + 1) * rows, :] for q in range(chunks)], axis=1
        )
        source[f] = 0.25 * (cond_gain[f] * rate - 0.5 * corr[:, f : f + 1] + deposit)

    row_id = lax.broadcasted_iota(jnp.int32, (rows, cols), 0)
    col_id = lax.broadcasted_iota(jnp.int32, (rows, cols), 1)
    row_low = jnp.where(sp == 0, 0.0, 1.0)
    row_high = jnp.where(sp == n_span - 1, 0.0, 1.0)
    col_low = jnp.where(me == 0, 0.0, 1.0)
    col_high = jnp.where(me == n_pitch - 1, 0.0, 1.0)

    def advance(u, f, turn):
        below = row_in[2 * turn + 1, f : f + 1, :] * row_low
        above = row_in[2 * turn, f : f + 1, :] * row_high
        before = col_in[2 * turn + 1][:, f : f + 1] * col_low
        after = col_in[2 * turn][:, f : f + 1] * col_high
        upper = jnp.where(row_id == rows - 1, above, pltpu.roll(u, rows - 1, axis=0))
        lower = jnp.where(row_id == 0, below, pltpu.roll(u, 1, axis=0))
        ahead = jnp.where(col_id == cols - 1, after, pltpu.roll(u, cols - 1, axis=1))
        behind = jnp.where(col_id == 0, before, pltpu.roll(u, 1, axis=1))
        return (
            u
            + source[f]
            + advection[0, f] * (upper - lower)
            + advection[1, f] * (ahead - behind)
            + nu[...] * (upper + lower + ahead + behind - 4.0 * u)
        )

    for copy in first_halo:
        copy.wait()
    left = jnp.zeros((rows, 128), F32)
    right = jnp.zeros((rows, 128), F32)
    for f in range(nf):
        u = advance(fields[f], f, 0)
        state[f] = u
        left = jnp.where(lane == f, u[:, 0:1], left)
        right = jnp.where(lane == f, u[:, cols - 1 : cols], right)
        row_out[2, f : f + 1, :] = u[0:1, :]
        row_out[3, f : f + 1, :] = u[rows - 1 : rows, :]
    col_out[2] = left
    col_out[3] = right
    second_halo = halo_copies(1)
    for copy in second_halo:
        copy.start()
    for copy in second_halo:
        copy.wait()
    for f in range(nf):
        new_fields[f] = advance(state[f], f, 1)

    own_copy.wait()

    def wait_parcels(k, _):
        parcel_copy(k).wait()
        return 0

    lax.fori_loop(1, n_pitch, wait_parcels, 0)


def local(
    fields, diffusivity, mixing, cond_gain, advection, parcels, cell, couple, relax, drag, counts
):
    nf, rows, cols = fields.shape
    nq, npar = parcels.shape
    n_pitch, n_span = lax.axis_size("pitch"), lax.axis_size("span")
    cap = 2 * npar // n_pitch
    vmem = pl.BlockSpec(memory_space=pltpu.VMEM)
    hbm = pl.BlockSpec(memory_space=pl.ANY)
    dma = pltpu.SemaphoreType.DMA
    return pl.pallas_call(
        functools.partial(step_kernel, n_pitch, n_span, cap),
        out_shape=(
            jax.ShapeDtypeStruct(fields.shape, F32),
            jax.ShapeDtypeStruct((nq, n_pitch * cap), F32),
        ),
        in_specs=[hbm] * 11,
        out_specs=(vmem, pl.BlockSpec(memory_space=pl.ANY)),
        scratch_shapes=[
            pltpu.SMEM((n_pitch,), jnp.int32),
            pltpu.SMEM((nf,), F32),
            pltpu.SMEM((2, nf), F32),
            pltpu.VMEM((npar // KB, KB // 128, 128), jnp.int32),
            pltpu.VMEM(fields.shape, F32),
            pltpu.VMEM((rows, cols), F32),
            pltpu.VMEM(mixing.shape, F32),
            pltpu.VMEM((nf, nq), F32),
            pltpu.VMEM((1, nq), F32),
            pltpu.VMEM((nf, nq), F32),
            dma((10,)),
            dma((npar // KB,)),
            pltpu.SMEM((n_pitch,), jnp.int32),
            pltpu.VMEM((nf * A, 2 * B), BF),
            pltpu.VMEM((nf * A, B), F32),
            pltpu.VMEM(((npar + KB) // 128, nq, 128), F32),
            pltpu.VMEM((npar // KB, nq, KB), F32),
            pltpu.VMEM((n_pitch, nq, cap), F32),
            pltpu.VMEM((n_span * rows, 128), F32),
            pltpu.VMEM(fields.shape, F32),
            pltpu.VMEM(fields.shape, F32),
            pltpu.VMEM((4, 8, cols), F32),
            pltpu.VMEM((4, 8, cols), F32),
            pltpu.VMEM((4, rows, 128), F32),
            pltpu.VMEM((4, rows, 128), F32),
            dma((n_pitch,)),
            dma((n_pitch,)),
            dma((n_span,)),
            dma((n_span,)),
            dma((8,)),
            dma((8,)),
            dma,
        ],
        compiler_params=pltpu.CompilerParams(
            collective_id=0, has_side_effects=True, vmem_limit_bytes=60 << 20
        ),
        cost_estimate=pl.CostEstimate(
            flops=8 * nf * rows * cols * npar, bytes_accessed=6 << 20, transcendentals=0
        ),
    )(
        counts,
        cond_gain,
        advection.T,
        cell.reshape(npar // KB, KB // 128, 128),
        fields,
        diffusivity,
        mixing,
        parcels,
        couple,
        relax.reshape(1, nq),
        drag.T,
    )


def solution(mesh):
    return jax.shard_map(
        local,
        mesh=mesh,
        in_specs=(
            P(None, "span", "pitch"),
            P("span", "pitch"),
            P(),
            P(),
            P(),
            P(None, ("pitch", "span")),
            P(("pitch", "span")),
            P(),
            P(),
            P(),
            P(("pitch", "span")),
        ),
        out_specs=(P(None, "span", "pitch"), P(None, ("pitch", "span"))),
        check_vma=False,
    )
```

```python
import functools

import jax
import jax.numpy as jnp
from jax import lax
from jax.experimental import pallas as pl
from jax.experimental.pallas import tpu as pltpu
from jax.sharding import PartitionSpec as P

F32, BF = jnp.float32, jnp.bfloat16
MESH = pl.DeviceIdType.MESH
AHEAD = 2
A, B, KB = 128, 512, 512


def step_kernel(
    n_pitch,
    n_span,
    cap,
    counts_hbm,
    gain_hbm,
    advection_hbm,
    cell_hbm,
    fields_hbm,
    nu_hbm,
    mixing_hbm,
    parcels_hbm,
    couple_hbm,
    relax_hbm,
    drag_hbm,
    new_fields,
    arrived,
    counts,
    cond_gain,
    advection,
    cell,
    fields,
    nu,
    mixing,
    couple,
    relax,
    drag,
    load_sem,
    record_sem,
    offs,
    table,
    place,
    place_s,
    place_sem,
    total,
    moved,
    records,
    outgoing,
    profile,
    source,
    state,
    row_out,
    row_in,
    col_out,
    col_in,
    send_sem,
    recv_sem,
    prof_send,
    prof_recv,
    halo_send,
    halo_recv,
    own_sem,
    out_sem,
):
    nf, rows, cols = fields.shape
    nq, npar = parcels_hbm.shape
    chunks = cols // B
    blocks = npar // KB
    me, sp = lax.axis_index("pitch"), lax.axis_index("span")
    pitch_next, pitch_prev = lax.rem(me + 1, n_pitch), lax.rem(me + n_pitch - 1, n_pitch)
    span_next, span_prev = lax.rem(sp + 1, n_span), lax.rem(sp + n_span - 1, n_span)

    loads = {}
    for n, (name, there, here) in enumerate(
        (
            ("counts", counts_hbm, counts),
            ("fields", fields_hbm, fields),
            ("cell", cell_hbm, cell),
            ("relax", relax_hbm, relax),
            ("drag", drag_hbm, drag),
            ("couple", couple_hbm, couple),
            ("mixing", mixing_hbm, mixing),
            ("nu", nu_hbm, nu),
            ("gain", gain_hbm, cond_gain),
            ("advection", advection_hbm, advection),
        )
    ):
        loads[name] = pltpu.make_async_copy(there, here, load_sem.at[n])
    for name in ("counts", "fields", "cell", "relax", "drag"):
        loads[name].start()
    record_loads = [
        pltpu.make_async_copy(
            parcels_hbm.at[:, s * KB : (s + 1) * KB], records.at[s], record_sem.at[s]
        )
        for s in range(blocks)
    ]
    for load in record_loads:
        load.start()
    for name in ("couple", "mixing", "nu", "gain", "advection"):
        loads[name].start()

    barrier = pltpu.get_barrier_semaphore()

    def greet_pitch(k, _):
        pl.semaphore_signal(
            barrier, inc=1, device_id=(lax.rem(me + k, n_pitch), sp), device_id_type=MESH
        )
        return 0

    def greet_span(k, _):
        pl.semaphore_signal(
            barrier, inc=1, device_id=(me, lax.rem(sp + k, n_span)), device_id_type=MESH
        )
        return 0

    lax.fori_loop(1, n_pitch, greet_pitch, 0)
    lax.fori_loop(1, n_span, greet_span, 0)

    loads["counts"].wait()
    running = jnp.int32(0)
    for p in range(n_pitch):
        offs[p] = running
        running = running + counts[p]
    first = offs[pitch_next] // KB
    loads["fields"].wait()

    loads["cell"].wait()
    lane_128 = lax.broadcasted_iota(jnp.int32, (KB // 128, 128), 1)
    for s in range(blocks):
        at = slice(s * (KB // 128), (s + 1) * (KB // 128))
        place[0, at, :] = cell[s] // 128
        place[1, at, :] = (lane_128 - cell[s]) & 127
    place_copy = pltpu.make_async_copy(place, place_s, place_sem)
    place_copy.start()

    for f in range(nf):
        for r in range(0, rows, 8):
            for q in range(cols // 128):
                at = pl.ds((r * (cols // 128) + q) * 8 + f, 8, stride=cols // 16)
                table[at, :] = fields[f, r : r + 8, q * 128 : (q + 1) * 128]
    tiles = table.reshape(rows * cols // 128, 8, 128)

    lane = lax.broadcasted_iota(jnp.int32, (rows, 128), 1)
    mean = jnp.zeros((rows, 128), F32)
    left = jnp.zeros((rows, 128), F32)
    right = jnp.zeros((rows, 128), F32)
    for f in range(nf):
        x = fields[f]
        mean = jnp.where(lane == f, jnp.sum(x, axis=1, keepdims=True) * (1.0 / cols), mean)
        left = jnp.where(lane == f, x[:, 0:1], left)
        right = jnp.where(lane == f, x[:, cols - 1 : cols], right)
        row_out[0, f : f + 1, :] = x[0:1, :]
        row_out[1, f : f + 1, :] = x[rows - 1 : rows, :]
    col_out[0] = left
    col_out[1] = right
    mine = pl.ds(pl.multiple_of(sp * rows, rows), rows)
    profile[mine, :] = mean

    diag = lax.broadcasted_iota(jnp.int32, (nq, nq), 0) == lax.broadcasted_iota(
        jnp.int32, (nq, nq), 1
    )

    def column(line):
        return jnp.sum(jnp.where(diag, line, 0.0), axis=1, keepdims=True)

    for name in ("relax", "drag", "couple"):
        loads[name].wait()
    keep = column(1.0 - relax[...])
    pull = [column(drag[f : f + 1, :]) for f in range(nf)]
    cp = couple[...]
    index_a = lax.broadcasted_iota(jnp.int32, (A, KB), 0)
    index_b = lax.broadcasted_iota(jnp.int32, (B, KB), 0)
    lane_8 = lax.broadcasted_iota(jnp.int32, (8, 128), 1)
    lane_q = lax.broadcasted_iota(jnp.int32, (nq, 128), 1)

    def block_of(s):
        return lax.rem(first + s, blocks)

    def cells_of(block):
        homes = cell[block]
        c = jnp.concatenate([homes[q : q + 1] for q in range(KB // 128)], axis=1)
        in_row = c & (cols - 1)
        hot_a = index_a == (in_row // B) * rows + c // cols
        hot_b = jnp.where(index_b == (in_row & (B - 1)), 1.0, 0.0).astype(BF)
        return hot_a, hot_b

    def gather(s):
        block = block_of(s)
        for h in range(KB // 128):
            row = block * (KB // 128) + h
            fluid = jnp.zeros((8, 128), F32)
            for j in range(128):
                found = pltpu.roll(tiles[place_s[0, row, j]], place_s[1, row, j], axis=1)
                fluid = jnp.where(lane_8 == j, found, fluid)
            value = keep * records[block, :, h * 128 : (h + 1) * 128]
            for f in range(nf):
                value = value + pull[f] * fluid[f : f + 1, :]
            moved[s * (KB // 128) + h] = value

    def pack(k, slot):
        p = lax.rem(me + k, n_pitch)
        count = counts[p]
        start = lax.rem(offs[p] - first * KB + npar, npar)
        tile = start // 128
        pieces = [moved[tile + q] for q in range(cap // 128 + 1)]
        shift = lax.rem(start, 128)
        turned = [pltpu.roll(piece, lax.rem(128 - shift, 128), axis=1) for piece in pieces]
        for q in range(cap // 128):
            piece = jnp.where(lane_q < 128 - shift, turned[q], turned[q + 1])
            outgoing[slot, :, q * 128 : (q + 1) * 128] = jnp.where(
                lane_q + q * 128 < count, piece, 0.0
            )

    own_slots = pl.ds(pl.multiple_of(me * cap, cap), cap)

    def parcel_copy(k):
        return pltpu.make_async_remote_copy(
            src_ref=outgoing.at[k],
            dst_ref=arrived.at[:, own_slots],
            send_sem=send_sem.at[k],
            recv_sem=recv_sem.at[k],
            device_id=(lax.rem(me + k, n_pitch), sp),
            device_id_type=MESH,
        )

    def profile_copy(k):
        return pltpu.make_async_remote_copy(
            src_ref=profile.at[mine],
            dst_ref=profile.at[mine],
            send_sem=prof_send.at[k],
            recv_sem=prof_recv.at[k],
            device_id=(me, lax.rem(sp + k, n_span)),
            device_id_type=MESH,
        )

    def halo_copies(turn):
        copies = []
        for side in range(2):
            for kind, (out, into, target) in enumerate(
                (
                    (row_out, row_in, (me, (span_prev, span_next)[side])),
                    (col_out, col_in, ((pitch_prev, pitch_next)[side], sp)),
                )
            ):
                copies.append(
                    pltpu.make_async_remote_copy(
                        src_ref=out.at[2 * turn + side],
                        dst_ref=into.at[2 * turn + side],
                        send_sem=halo_send.at[4 * turn + 2 * side + kind],
                        recv_sem=halo_recv.at[4 * turn + 2 * side + kind],
                        device_id=target,
                        device_id_type=MESH,
                    )
                )
        return copies

    for load in record_loads:
        load.wait()
    place_copy.wait()
    total[...] = jnp.zeros_like(total)
    pl.semaphore_wait(barrier, n_pitch + n_span - 2)

    def start_profile(k, _):
        profile_copy(k).start()
        return 0

    lax.fori_loop(1, n_span, start_profile, 0)
    first_halo = halo_copies(0)
    for copy in first_halo:
        copy.start()

    def scatter(s):
        block = block_of(s)
        hot_a, hot_b = cells_of(block)
        par = records[block]
        given = jnp.zeros((nf, KB), F32)
        for q in range(nq):
            given = given + cp[:, q : q + 1] * par[q : q + 1, :]
        hi = given.astype(BF).astype(F32)
        lo = given - hi
        spread = jnp.concatenate(
            [
                jnp.concatenate(
                    [jnp.where(hot_a, x[f : f + 1], 0.0).astype(BF) for f in range(nf)], axis=0
                )
                for x in (hi, lo)
            ],
            axis=1,
        )
        total[...] += lax.dot_general(
            spread,
            jnp.concatenate([hot_b, hot_b], axis=1),
            (((1,), (1,)), ((), ())),
            preferred_element_type=F32,
        )

    def work(s, _):
        gather(s)
        scatter(s)
        pack(s, s)

        @pl.when(s >= 1)
        def _():
            parcel_copy(s).start()

        return 0

    lax.fori_loop(0, blocks, work, 0)
    for q in range(KB // 128):
        moved[npar // 128 + q] = moved[q]

    def send(k, _):
        pack(k, k)
        parcel_copy(k).start()
        return 0

    lax.fori_loop(blocks, blocks + AHEAD, send, 0)

    def wait_profile(k, _):
        profile_copy(k).wait()
        return 0

    lax.fori_loop(1, n_span, wait_profile, 0)
    for name in ("mixing", "nu", "gain", "advection"):
        loads[name].wait()
    corr = jnp.dot(
        mixing[mine, :], profile[...], precision=lax.Precision.HIGHEST, preferred_element_type=F32
    )
    x = fields[0] + corr[:, 0:1]
    rate = (jnp.maximum(x, 0.0) + jnp.log1p(jnp.exp(-jnp.abs(x)))) * (
        1.0 + jnp.tanh(fields[1] + corr[:, 1:2])
    )
    source[0] = rate
    for f in reversed(range(nf)):
        deposit = jnp.concatenate(
            [total[f * A + q * rows : f * A + (q + 1) * rows, :] for q in range(chunks)], axis=1
        )
        source[f] = 0.25 * (cond_gain[f] * rate - 0.5 * corr[:, f : f + 1] + deposit)

    row_id = lax.broadcasted_iota(jnp.int32, (rows, cols), 0)
    col_id = lax.broadcasted_iota(jnp.int32, (rows, cols), 1)
    row_low = jnp.where(sp == 0, 0.0, 1.0)
    row_high = jnp.where(sp == n_span - 1, 0.0, 1.0)
    col_low = jnp.where(me == 0, 0.0, 1.0)
    col_high = jnp.where(me == n_pitch - 1, 0.0, 1.0)

    def advance(u, f, turn):
        below = row_in[2 * turn + 1, f : f + 1, :] * row_low
        above = row_in[2 * turn, f : f + 1, :] * row_high
        before = col_in[2 * turn + 1][:, f : f + 1] * col_low
        after = col_in[2 * turn][:, f : f + 1] * col_high
        upper = jnp.where(row_id == rows - 1, above, pltpu.roll(u, rows - 1, axis=0))
        lower = jnp.where(row_id == 0, below, pltpu.roll(u, 1, axis=0))
        ahead = jnp.where(col_id == cols - 1, after, pltpu.roll(u, cols - 1, axis=1))
        behind = jnp.where(col_id == 0, before, pltpu.roll(u, 1, axis=1))
        return (
            u
            + source[f]
            + advection[0, f] * (upper - lower)
            + advection[1, f] * (ahead - behind)
            + nu[...] * (upper + lower + ahead + behind - 4.0 * u)
        )

    for copy in first_halo:
        copy.wait()
    left = jnp.zeros((rows, 128), F32)
    right = jnp.zeros((rows, 128), F32)
    for f in range(nf):
        u = advance(fields[f], f, 0)
        state[f] = u
        left = jnp.where(lane == f, u[:, 0:1], left)
        right = jnp.where(lane == f, u[:, cols - 1 : cols], right)
        row_out[2, f : f + 1, :] = u[0:1, :]
        row_out[3, f : f + 1, :] = u[rows - 1 : rows, :]
    col_out[2] = left
    col_out[3] = right
    second_halo = halo_copies(1)
    for copy in second_halo:
        copy.start()
    lax.fori_loop(blocks + AHEAD, n_pitch, send, 0)
    pack(n_pitch, 0)
    own_copy = pltpu.make_async_copy(outgoing.at[0], arrived.at[:, own_slots], own_sem)
    own_copy.start()

    for copy in second_halo:
        copy.wait()
    for f in range(nf):
        fields[f] = advance(state[f], f, 1)
        pltpu.make_async_copy(fields.at[f], new_fields.at[f], out_sem.at[f]).start()
    for f in range(nf):
        pltpu.make_async_copy(fields.at[f], new_fields.at[f], out_sem.at[f]).wait()

    own_copy.wait()

    def wait_parcels(k, _):
        parcel_copy(k).wait()
        return 0

    lax.fori_loop(1, n_pitch, wait_parcels, 0)


def hand_over_kernel(fields_from, arrived_from, fields_to, arrived_to, held, slots, sem_a, sem_b):
    parts = sem_b.shape[1]
    width = slots.shape[1] // parts
    ways = [
        (fields_from.at[f], held.at[f], fields_to.at[f], sem_a.at[0, f], sem_a.at[1, f])
        for f in range(held.shape[0])
    ]
    for q in range(parts):
        at = slice(q * width, (q + 1) * width)
        ways.append(
            (
                arrived_from.at[:, at],
                slots.at[:, at],
                arrived_to.at[:, at],
                sem_b.at[0, q],
                sem_b.at[1, q],
            )
        )
    into = [pltpu.make_async_copy(a, b, s) for a, b, _, s, _ in ways]
    out = [pltpu.make_async_copy(b, c, s) for _, b, c, _, s in ways]
    for copy in into:
        copy.start()
    for first, second in zip(into, out):
        first.wait()
        second.start()
    for copy in out:
        copy.wait()


def local(
    fields, diffusivity, mixing, cond_gain, advection, parcels, cell, couple, relax, drag, counts
):
    nf, rows, cols = fields.shape
    nq, npar = parcels.shape
    n_pitch, n_span = lax.axis_size("pitch"), lax.axis_size("span")
    cap = 2 * npar // n_pitch
    hbm = pl.BlockSpec(memory_space=pl.ANY)
    dma = pltpu.SemaphoreType.DMA
    results = pl.pallas_call(
        functools.partial(step_kernel, n_pitch, n_span, cap),
        out_shape=(
            jax.ShapeDtypeStruct(fields.shape, F32),
            jax.ShapeDtypeStruct((nq, n_pitch * cap), F32),
        ),
        in_specs=[hbm] * 11,
        out_specs=(hbm, hbm),
        scratch_shapes=[
            pltpu.SMEM((n_pitch,), jnp.int32),
            pltpu.SMEM((nf,), F32),
            pltpu.SMEM((2, nf), F32),
            pltpu.VMEM((npar // KB, KB // 128, 128), jnp.int32),
            pltpu.VMEM(fields.shape, F32),
            pltpu.VMEM((rows, cols), F32),
            pltpu.VMEM(mixing.shape, F32),
            pltpu.VMEM((nf, nq), F32),
            pltpu.VMEM((1, nq), F32),
            pltpu.VMEM((nf, nq), F32),
            dma((10,)),
            dma((npar // KB,)),
            pltpu.SMEM((n_pitch,), jnp.int32),
            pltpu.VMEM((rows * cols // 16, 128), F32),
            pltpu.VMEM((2, npar // 128, 128), jnp.int32),
            pltpu.SMEM((2, npar // 128, 128), jnp.int32),
            dma,
            pltpu.VMEM((nf * A, B), F32),
            pltpu.VMEM(((npar + KB) // 128, nq, 128), F32),
            pltpu.VMEM((npar // KB, nq, KB), F32),
            pltpu.VMEM((n_pitch, nq, cap), F32),
            pltpu.VMEM((n_span * rows, 128), F32),
            pltpu.VMEM(fields.shape, F32),
            pltpu.VMEM(fields.shape, F32),
            pltpu.VMEM((4, 8, cols), F32),
            pltpu.VMEM((4, 8, cols), F32),
            pltpu.VMEM((4, rows, 128), F32),
            pltpu.VMEM((4, rows, 128), F32),
            dma((n_pitch,)),
            dma((n_pitch,)),
            dma((n_span,)),
            dma((n_span,)),
            dma((8,)),
            dma((8,)),
            dma,
            dma((nf,)),
        ],
        compiler_params=pltpu.CompilerParams(
            collective_id=0, has_side_effects=True, vmem_limit_bytes=60 << 20
        ),
        cost_estimate=pl.CostEstimate(
            flops=8 * nf * rows * cols * npar, bytes_accessed=6 << 20, transcendentals=0
        ),
    )(
        counts,
        cond_gain,
        advection.T,
        cell.reshape(npar // KB, KB // 128, 128),
        fields,
        diffusivity,
        mixing,
        parcels,
        couple,
        relax.reshape(1, nq),
        drag.T,
    )
    return pl.pallas_call(
        hand_over_kernel,
        out_shape=tuple(jax.ShapeDtypeStruct(x.shape, x.dtype) for x in results),
        in_specs=[hbm] * 2,
        out_specs=(hbm, hbm),
        scratch_shapes=[
            pltpu.VMEM(results[0].shape, F32),
            pltpu.VMEM(results[1].shape, F32),
            dma((2, nf)),
            dma((2, 8)),
        ],
        compiler_params=pltpu.CompilerParams(vmem_limit_bytes=60 << 20),
    )(*results)


def solution(mesh):
    return jax.shard_map(
        local,
        mesh=mesh,
        in_specs=(
            P(None, "span", "pitch"),
            P("span", "pitch"),
            P(),
            P(),
            P(),
            P(None, ("pitch", "span")),
            P(("pitch", "span")),
            P(),
            P(),
            P(),
            P(("pitch", "span")),
        ),
        out_specs=(P(None, "span", "pitch"), P(None, ("pitch", "span"))),
        check_vma=False,
    )
```

```python
import functools

import jax
import jax.numpy as jnp
from jax import lax
from jax.experimental import pallas as pl
from jax.experimental.pallas import tpu as pltpu
from jax.sharding import PartitionSpec as P

F32, BF = jnp.float32, jnp.bfloat16
MESH = pl.DeviceIdType.MESH
ALONE = 12
AHEAD = 2
EACH = 2
A, B, KB = 128, 512, 512


def step_kernel(
    n_pitch,
    n_span,
    cap,
    counts_hbm,
    gain_hbm,
    advection_hbm,
    cell_hbm,
    fields_hbm,
    nu_hbm,
    mixing_hbm,
    parcels_hbm,
    couple_hbm,
    relax_hbm,
    drag_hbm,
    new_fields,
    arrived,
    counts,
    cond_gain,
    advection,
    cell,
    fields,
    nu,
    mixing,
    couple,
    relax,
    drag,
    load_sem,
    record_sem,
    offs,
    table,
    pair,
    corr,
    rate,
    place,
    place_s,
    place_sem,
    total,
    moved,
    records,
    outgoing,
    profile,
    source,
    state,
    row_out,
    row_in,
    col_out,
    col_in,
    send_sem,
    recv_sem,
    prof_send,
    prof_recv,
    halo_send,
    halo_recv,
    own_sem,
    out_sem,
):
    nf, rows, cols = fields.shape
    nq, npar = parcels_hbm.shape
    chunks = cols // B
    blocks = npar // KB
    me, sp = lax.axis_index("pitch"), lax.axis_index("span")
    pitch_next, pitch_prev = lax.rem(me + 1, n_pitch), lax.rem(me + n_pitch - 1, n_pitch)
    span_next, span_prev = lax.rem(sp + 1, n_span), lax.rem(sp + n_span - 1, n_span)

    loads = {}
    for n, (name, there, here) in enumerate(
        (
            ("counts", counts_hbm, counts),
            ("fields", fields_hbm, fields),
            ("cell", cell_hbm, cell),
            ("relax", relax_hbm, relax),
            ("drag", drag_hbm, drag),
            ("couple", couple_hbm, couple),
            ("mixing", mixing_hbm, mixing),
            ("nu", nu_hbm, nu),
            ("gain", gain_hbm, cond_gain),
            ("advection", advection_hbm, advection),
        )
    ):
        loads[name] = pltpu.make_async_copy(there, here, load_sem.at[n])
    for name in ("cell", "counts", "fields", "relax", "drag"):
        loads[name].start()
    record_loads = [
        pltpu.make_async_copy(
            parcels_hbm.at[:, s * KB : (s + 1) * KB], records.at[s], record_sem.at[s]
        )
        for s in range(blocks)
    ]
    for load in record_loads:
        load.start()
    for name in ("couple", "mixing", "nu", "gain", "advection"):
        loads[name].start()

    barrier = pltpu.get_barrier_semaphore()

    def greet_pitch(k, _):
        pl.semaphore_signal(
            barrier, inc=1, device_id=(lax.rem(me + k, n_pitch), sp), device_id_type=MESH
        )
        return 0

    def greet_span(k, _):
        pl.semaphore_signal(
            barrier, inc=1, device_id=(me, lax.rem(sp + k, n_span)), device_id_type=MESH
        )
        return 0

    lax.fori_loop(1, n_pitch, greet_pitch, 0)
    lax.fori_loop(1, n_span, greet_span, 0)

    loads["cell"].wait()
    lane_128 = lax.broadcasted_iota(jnp.int32, (KB // 128, 128), 1)
    for s in range(blocks):
        at = slice(s * (KB // 128), (s + 1) * (KB // 128))
        place[0, at, :] = cell[s] // 128
        place[1, at, :] = (lane_128 - cell[s]) & 127
    place_copy = pltpu.make_async_copy(place, place_s, place_sem)
    place_copy.start()

    loads["counts"].wait()
    running = jnp.int32(0)
    for p in range(n_pitch):
        offs[p] = running
        running = running + counts[p]
    first = offs[pitch_next] // KB
    loads["fields"].wait()

    for f in range(nf):
        for r in range(0, rows, 8):
            for q in range(cols // 128):
                at = pl.ds((r * (cols // 128) + q) * 8 + f, 8, stride=cols // 16)
                table[at, :] = fields[f, r : r + 8, q * 128 : (q + 1) * 128]
    for f in range(nf):
        for q in range(chunks):
            x = fields[f, :, q * B : (q + 1) * B]
            hi = x.astype(BF)
            at = f * A + q * rows
            pair[at : at + rows, 0:B] = hi
            pair[at : at + rows, B : 2 * B] = (x - hi.astype(F32)).astype(BF)
    tiles = table.reshape(rows * cols // 128, 8, 128)

    lane = lax.broadcasted_iota(jnp.int32, (rows, 128), 1)
    mean = jnp.zeros((rows, 128), F32)
    left = jnp.zeros((rows, 128), F32)
    right = jnp.zeros((rows, 128), F32)
    for f in range(nf):
        x = fields[f]
        mean = jnp.where(lane == f, jnp.sum(x, axis=1, keepdims=True) * (1.0 / cols), mean)
        left = jnp.where(lane == f, x[:, 0:1], left)
        right = jnp.where(lane == f, x[:, cols - 1 : cols], right)
        row_out[0, f : f + 1, :] = x[0:1, :]
        row_out[1, f : f + 1, :] = x[rows - 1 : rows, :]
    col_out[0] = left
    col_out[1] = right
    mine = pl.ds(pl.multiple_of(sp * rows, rows), rows)
    profile[mine, :] = mean

    diag = lax.broadcasted_iota(jnp.int32, (nq, nq), 0) == lax.broadcasted_iota(
        jnp.int32, (nq, nq), 1
    )

    def column(line):
        return jnp.sum(jnp.where(diag, line, 0.0), axis=1, keepdims=True)

    for name in ("relax", "drag", "couple"):
        loads[name].wait()
    keep = column(1.0 - relax[...])
    pull = [column(drag[f : f + 1, :]) for f in range(nf)]
    cp = couple[...]
    index_a = lax.broadcasted_iota(jnp.int32, (A, KB), 0)
    index_b = lax.broadcasted_iota(jnp.int32, (B, KB), 0)
    lane_8 = lax.broadcasted_iota(jnp.int32, (8, 128), 1)
    lane_q = lax.broadcasted_iota(jnp.int32, (nq, 128), 1)

    def block_of(s):
        return lax.rem(first + s, blocks)

    def cells_of(block, low):
        homes = cell[block]
        c = jnp.concatenate([homes[q : q + 1] for q in range(low, KB // 128)], axis=1)
        in_row = c & (cols - 1)
        hot_a = index_a[:, low * 128 :] == (in_row // B) * rows + c // cols
        hot_b = jnp.where(index_b[:, low * 128 :] == (in_row & (B - 1)), 1.0, 0.0).astype(BF)
        return hot_a, hot_b

    def gather_by_matmul(s, low):
        block = block_of(s)
        hot_a, hot_b = cells_of(block, low)
        picked = jnp.dot(
            pair[...], jnp.concatenate([hot_b, hot_b], axis=0), preferred_element_type=F32
        )
        value = keep * records[block, :, low * 128 :]
        for f in range(nf):
            fluid = jnp.sum(
                jnp.where(hot_a, picked[f * A : (f + 1) * A], 0.0), axis=0, keepdims=True
            )
            value = value + pull[f] * fluid
        for q in range(low, KB // 128):
            moved[s * (KB // 128) + q] = value[:, (q - low) * 128 : (q - low + 1) * 128]

    def gather(s, high):
        block = block_of(s)
        for h in range(high):
            row = block * (KB // 128) + h
            fluid = jnp.zeros((8, 128), F32)
            for j in range(128):
                found = pltpu.roll(tiles[place_s[0, row, j]], place_s[1, row, j], axis=1)
                fluid = jnp.where(lane_8 == j, found, fluid)
            value = keep * records[block, :, h * 128 : (h + 1) * 128]
            for f in range(nf):
                value = value + pull[f] * fluid[f : f + 1, :]
            moved[s * (KB // 128) + h] = value

    def pack(k, slot):
        p = lax.rem(me + k, n_pitch)
        count = counts[p]
        start = lax.rem(offs[p] - first * KB + npar, npar)
        tile = start // 128
        pieces = [moved[tile + q] for q in range(cap // 128 + 1)]
        shift = lax.rem(start, 128)
        turned = [pltpu.roll(piece, lax.rem(128 - shift, 128), axis=1) for piece in pieces]
        for q in range(cap // 128):
            piece = jnp.where(lane_q < 128 - shift, turned[q], turned[q + 1])
            outgoing[slot, :, q * 128 : (q + 1) * 128] = jnp.where(
                lane_q + q * 128 < count, piece, 0.0
            )

    own_slots = pl.ds(pl.multiple_of(me * cap, cap), cap)

    def parcel_copy(k):
        return pltpu.make_async_remote_copy(
            src_ref=outgoing.at[k],
            dst_ref=arrived.at[:, own_slots],
            send_sem=send_sem.at[k],
            recv_sem=recv_sem.at[k],
            device_id=(lax.rem(me + k, n_pitch), sp),
            device_id_type=MESH,
        )

    def profile_copy(k):
        return pltpu.make_async_remote_copy(
            src_ref=profile.at[mine],
            dst_ref=profile.at[mine],
            send_sem=prof_send.at[k],
            recv_sem=prof_recv.at[k],
            device_id=(me, lax.rem(sp + k, n_span)),
            device_id_type=MESH,
        )

    def halo_copies(turn):
        copies = []
        for side in range(2):
            for kind, (out, into, target) in enumerate(
                (
                    (row_out, row_in, (me, (span_prev, span_next)[side])),
                    (col_out, col_in, ((pitch_prev, pitch_next)[side], sp)),
                )
            ):
                copies.append(
                    pltpu.make_async_remote_copy(
                        src_ref=out.at[2 * turn + side],
                        dst_ref=into.at[2 * turn + side],
                        send_sem=halo_send.at[4 * turn + 2 * side + kind],
                        recv_sem=halo_recv.at[4 * turn + 2 * side + kind],
                        device_id=target,
                        device_id_type=MESH,
                    )
                )
        return copies

    for load in record_loads:
        load.wait()
    place_copy.wait()
    total[...] = jnp.zeros_like(total)

    def start_profile(k, _):
        profile_copy(k).start()
        return 0

    first_halo = halo_copies(0)

    def scatter(steps):
        left_side, right_side = [], []
        for s in steps:
            block = block_of(s)
            hot_a, hot_b = cells_of(block, 0)
            par = records[block]
            given = jnp.zeros((nf, KB), F32)
            for q in range(nq):
                given = given + cp[:, q : q + 1] * par[q : q + 1, :]
            hi = given.astype(BF).astype(F32)
            lo = given - hi
            for x in (hi, lo):
                left_side.append(
                    jnp.concatenate(
                        [jnp.where(hot_a, x[f : f + 1], 0.0).astype(BF) for f in range(nf)],
                        axis=0,
                    )
                )
                right_side.append(hot_b)
        total[...] += lax.dot_general(
            jnp.concatenate(left_side, axis=1),
            jnp.concatenate(right_side, axis=1),
            (((1,), (1,)), ((), ())),
            preferred_element_type=F32,
        )

    def wait_profile(k, _):
        profile_copy(k).wait()
        return 0

    def rate_of(part, parts):
        at = pl.ds(pl.multiple_of(part * (cols // parts), cols // parts), cols // parts)
        x = fields[0, :, at] + corr[:, 0:1]
        rate[:, at] = (jnp.maximum(x, 0.0) + jnp.log1p(jnp.exp(-jnp.abs(x)))) * (
            1.0 + jnp.tanh(fields[1, :, at] + corr[:, 1:2])
        )

    def gather_only(s, _):
        gather(s, KB // 256)
        gather_by_matmul(s, KB // 256)
        pack(s, s)

        @pl.when(s == 0)
        def _():
            pl.semaphore_wait(barrier, n_pitch + n_span - 2)
            lax.fori_loop(1, n_span, start_profile, 0)
            for copy in first_halo:
                copy.start()

        @pl.when(s >= 1)
        def _():
            parcel_copy(s).start()

        return 0

    lax.fori_loop(0, ALONE, gather_only, 0)
    for name in ("mixing", "nu", "gain", "advection"):
        loads[name].wait()
    lax.fori_loop(1, n_span, wait_profile, 0)
    corr[...] = jnp.dot(
        mixing[mine, :], profile[...], precision=lax.Precision.HIGHEST, preferred_element_type=F32
    )

    def gather_and_scatter(s, _):
        gather(s, KB // 128)
        scatter([s])
        pack(s, s)
        parcel_copy(s).start()
        rate_of(s - ALONE, blocks - ALONE)
        return 0

    lax.fori_loop(ALONE, blocks, gather_and_scatter, 0)
    for q in range(KB // 128):
        moved[npar // 128 + q] = moved[q]

    def send(k, _):
        pack(k, k)
        parcel_copy(k).start()
        return 0

    lax.fori_loop(blocks, blocks + AHEAD, send, 0)

    def scatter_rest(t, _):
        scatter([2 * t, 2 * t + 1])
        for n in range(EACH):
            send(blocks + AHEAD + EACH * t + n, 0)
        return 0

    lax.fori_loop(0, ALONE // 2, scatter_rest, 0)

    for f in range(nf):
        deposit = jnp.concatenate(
            [total[f * A + q * rows : f * A + (q + 1) * rows, :] for q in range(chunks)], axis=1
        )
        source[f] = 0.25 * (cond_gain[f] * rate[...] - 0.5 * corr[:, f : f + 1] + deposit)

    row_id = lax.broadcasted_iota(jnp.int32, (rows, cols), 0)
    col_id = lax.broadcasted_iota(jnp.int32, (rows, cols), 1)
    row_low = jnp.where(sp == 0, 0.0, 1.0)
    row_high = jnp.where(sp == n_span - 1, 0.0, 1.0)
    col_low = jnp.where(me == 0, 0.0, 1.0)
    col_high = jnp.where(me == n_pitch - 1, 0.0, 1.0)

    def advance(u, f, turn):
        below = row_in[2 * turn + 1, f : f + 1, :] * row_low
        above = row_in[2 * turn, f : f + 1, :] * row_high
        before = col_in[2 * turn + 1][:, f : f + 1] * col_low
        after = col_in[2 * turn][:, f : f + 1] * col_high
        upper = jnp.where(row_id == rows - 1, above, pltpu.roll(u, rows - 1, axis=0))
        lower = jnp.where(row_id == 0, below, pltpu.roll(u, 1, axis=0))
        ahead = jnp.where(col_id == cols - 1, after, pltpu.roll(u, cols - 1, axis=1))
        behind = jnp.where(col_id == 0, before, pltpu.roll(u, 1, axis=1))
        return (
            u
            + source[f]
            + advection[0, f] * (upper - lower)
            + advection[1, f] * (ahead - behind)
            + nu[...] * (upper + lower + ahead + behind - 4.0 * u)
        )

    for copy in first_halo:
        copy.wait()
    left = jnp.zeros((rows, 128), F32)
    right = jnp.zeros((rows, 128), F32)
    for f in range(nf):
        u = advance(fields[f], f, 0)
        state[f] = u
        left = jnp.where(lane == f, u[:, 0:1], left)
        right = jnp.where(lane == f, u[:, cols - 1 : cols], right)
        row_out[2, f : f + 1, :] = u[0:1, :]
        row_out[3, f : f + 1, :] = u[rows - 1 : rows, :]
    col_out[2] = left
    col_out[3] = right
    second_halo = halo_copies(1)
    for copy in second_halo:
        copy.start()
    lax.fori_loop(blocks + AHEAD + EACH * (ALONE // 2), n_pitch, send, 0)
    pack(n_pitch, 0)
    own_copy = pltpu.make_async_copy(outgoing.at[0], arrived.at[:, own_slots], own_sem)
    own_copy.start()

    for copy in second_halo:
        copy.wait()
    for f in range(nf):
        fields[f] = advance(state[f], f, 1)
        pltpu.make_async_copy(fields.at[f], new_fields.at[f], out_sem.at[f]).start()
    for f in range(nf):
        pltpu.make_async_copy(fields.at[f], new_fields.at[f], out_sem.at[f]).wait()

    own_copy.wait()

    def wait_parcels(k, _):
        parcel_copy(k).wait()
        return 0

    lax.fori_loop(1, n_pitch, wait_parcels, 0)


def hand_over_kernel(fields_from, arrived_from, fields_to, arrived_to, held, slots, sem_a, sem_b):
    parts = sem_b.shape[1]
    width = slots.shape[1] // parts
    ways = [
        (fields_from.at[f], held.at[f], fields_to.at[f], sem_a.at[0, f], sem_a.at[1, f])
        for f in range(held.shape[0])
    ]
    for q in range(parts):
        at = slice(q * width, (q + 1) * width)
        ways.append(
            (
                arrived_from.at[:, at],
                slots.at[:, at],
                arrived_to.at[:, at],
                sem_b.at[0, q],
                sem_b.at[1, q],
            )
        )
    into = [pltpu.make_async_copy(a, b, s) for a, b, _, s, _ in ways]
    out = [pltpu.make_async_copy(b, c, s) for _, b, c, _, s in ways]
    for copy in into:
        copy.start()
    for first, second in zip(into, out):
        first.wait()
        second.start()
    for copy in out:
        copy.wait()


def local(
    fields, diffusivity, mixing, cond_gain, advection, parcels, cell, couple, relax, drag, counts
):
    nf, rows, cols = fields.shape
    nq, npar = parcels.shape
    n_pitch, n_span = lax.axis_size("pitch"), lax.axis_size("span")
    cap = 2 * npar // n_pitch
    hbm = pl.BlockSpec(memory_space=pl.ANY)
    dma = pltpu.SemaphoreType.DMA
    results = pl.pallas_call(
        functools.partial(step_kernel, n_pitch, n_span, cap),
        out_shape=(
            jax.ShapeDtypeStruct(fields.shape, F32),
            jax.ShapeDtypeStruct((nq, n_pitch * cap), F32),
        ),
        in_specs=[hbm] * 11,
        out_specs=(hbm, hbm),
        scratch_shapes=[
            pltpu.SMEM((n_pitch,), jnp.int32),
            pltpu.SMEM((nf,), F32),
            pltpu.SMEM((2, nf), F32),
            pltpu.VMEM((npar // KB, KB // 128, 128), jnp.int32),
            pltpu.VMEM(fields.shape, F32),
            pltpu.VMEM((rows, cols), F32),
            pltpu.VMEM(mixing.shape, F32),
            pltpu.VMEM((nf, nq), F32),
            pltpu.VMEM((1, nq), F32),
            pltpu.VMEM((nf, nq), F32),
            dma((10,)),
            dma((npar // KB,)),
            pltpu.SMEM((n_pitch,), jnp.int32),
            pltpu.VMEM((rows * cols // 16, 128), F32),
            pltpu.VMEM((nf * A, 2 * B), BF),
            pltpu.VMEM((rows, 128), F32),
            pltpu.VMEM((rows, cols), F32),
            pltpu.VMEM((2, npar // 128, 128), jnp.int32),
            pltpu.SMEM((2, npar // 128, 128), jnp.int32),
            dma,
            pltpu.VMEM((nf * A, B), F32),
            pltpu.VMEM(((npar + KB) // 128, nq, 128), F32),
            pltpu.VMEM((npar // KB, nq, KB), F32),
            pltpu.VMEM((n_pitch, nq, cap), F32),
            pltpu.VMEM((n_span * rows, 128), F32),
            pltpu.VMEM(fields.shape, F32),
            pltpu.VMEM(fields.shape, F32),
            pltpu.VMEM((4, 8, cols), F32),
            pltpu.VMEM((4, 8, cols), F32),
            pltpu.VMEM((4, rows, 128), F32),
            pltpu.VMEM((4, rows, 128), F32),
            dma((n_pitch,)),
            dma((n_pitch,)),
            dma((n_span,)),
            dma((n_span,)),
            dma((8,)),
            dma((8,)),
            dma,
            dma((nf,)),
        ],
        compiler_params=pltpu.CompilerParams(
            collective_id=0, has_side_effects=True, vmem_limit_bytes=60 << 20
        ),
        cost_estimate=pl.CostEstimate(
            flops=8 * nf * rows * cols * npar, bytes_accessed=6 << 20, transcendentals=0
        ),
    )(
        counts,
        cond_gain,
        advection.T,
        cell.reshape(npar // KB, KB // 128, 128),
        fields,
        diffusivity,
        mixing,
        parcels,
        couple,
        relax.reshape(1, nq),
        drag.T,
    )
    return pl.pallas_call(
        hand_over_kernel,
        out_shape=tuple(jax.ShapeDtypeStruct(x.shape, x.dtype) for x in results),
        in_specs=[hbm] * 2,
        out_specs=(hbm, hbm),
        scratch_shapes=[
            pltpu.VMEM(results[0].shape, F32),
            pltpu.VMEM(results[1].shape, F32),
            dma((2, nf)),
            dma((2, 8)),
        ],
        compiler_params=pltpu.CompilerParams(vmem_limit_bytes=60 << 20),
    )(*results)


def solution(mesh):
    return jax.shard_map(
        local,
        mesh=mesh,
        in_specs=(
            P(None, "span", "pitch"),
            P("span", "pitch"),
            P(),
            P(),
            P(),
            P(None, ("pitch", "span")),
            P(("pitch", "span")),
            P(),
            P(),
            P(),
            P(("pitch", "span")),
        ),
        out_specs=(P(None, "span", "pitch"), P(None, ("pitch", "span"))),
        check_vma=False,
    )
```

```python
import functools

import jax
import jax.numpy as jnp
from jax import lax
from jax.experimental import pallas as pl
from jax.experimental.pallas import tpu as pltpu
from jax.sharding import PartitionSpec as P

F32, BF = jnp.float32, jnp.bfloat16
MESH = pl.DeviceIdType.MESH
ALONE = 12
AHEAD = 2
EACH = 2
A, B, KB = 128, 512, 512


def step_kernel(
    n_pitch,
    n_span,
    cap,
    counts_hbm,
    gain_hbm,
    advection_hbm,
    cell_hbm,
    fields_hbm,
    nu_hbm,
    mixing_hbm,
    parcels_hbm,
    couple_hbm,
    relax_hbm,
    drag_hbm,
    new_fields,
    arrived,
    counts,
    cond_gain,
    advection,
    cell,
    fields,
    nu,
    mixing,
    couple,
    relax,
    drag,
    load_sem,
    record_sem,
    offs,
    table,
    pair,
    corr,
    rate,
    place,
    place_s,
    place_sem,
    total,
    moved,
    records,
    outgoing,
    profile,
    source,
    state,
    row_out,
    row_in,
    col_out,
    col_in,
    send_sem,
    recv_sem,
    prof_send,
    prof_recv,
    halo_send,
    halo_recv,
    own_sem,
    out_sem,
):
    nf, rows, cols = fields.shape
    nq, npar = parcels_hbm.shape
    chunks = cols // B
    blocks = npar // KB
    me, sp = lax.axis_index("pitch"), lax.axis_index("span")
    pitch_next, pitch_prev = lax.rem(me + 1, n_pitch), lax.rem(me + n_pitch - 1, n_pitch)
    span_next, span_prev = lax.rem(sp + 1, n_span), lax.rem(sp + n_span - 1, n_span)

    loads = {}
    for n, (name, there, here) in enumerate(
        (
            ("counts", counts_hbm, counts),
            ("fields", fields_hbm, fields),
            ("cell", cell_hbm, cell),
            ("relax", relax_hbm, relax),
            ("drag", drag_hbm, drag),
            ("couple", couple_hbm, couple),
            ("mixing", mixing_hbm, mixing),
            ("nu", nu_hbm, nu),
            ("gain", gain_hbm, cond_gain),
            ("advection", advection_hbm, advection),
        )
    ):
        loads[name] = pltpu.make_async_copy(there, here, load_sem.at[n])
    for name in ("cell", "counts", "fields", "relax", "drag"):
        loads[name].start()
    record_loads = [
        pltpu.make_async_copy(
            parcels_hbm.at[:, s * KB : (s + 1) * KB], records.at[s], record_sem.at[s]
        )
        for s in range(blocks)
    ]
    for load in record_loads:
        load.start()
    for name in ("couple", "mixing", "nu", "gain", "advection"):
        loads[name].start()

    barrier = pltpu.get_barrier_semaphore()

    def greet_pitch(k, _):
        pl.semaphore_signal(
            barrier, inc=1, device_id=(lax.rem(me + k, n_pitch), sp), device_id_type=MESH
        )
        return 0

    def greet_span(k, _):
        pl.semaphore_signal(
            barrier, inc=1, device_id=(me, lax.rem(sp + k, n_span)), device_id_type=MESH
        )
        return 0

    lax.fori_loop(1, n_pitch, greet_pitch, 0)
    lax.fori_loop(1, n_span, greet_span, 0)

    loads["cell"].wait()
    lane_128 = lax.broadcasted_iota(jnp.int32, (KB // 128, 128), 1)
    for s in range(blocks):
        at = slice(s * (KB // 128), (s + 1) * (KB // 128))
        place[0, at, :] = cell[s] // 128
        place[1, at, :] = (lane_128 - cell[s]) & 127
    place_copy = pltpu.make_async_copy(place, place_s, place_sem)
    place_copy.start()

    loads["counts"].wait()
    running = jnp.int32(0)
    for p in range(n_pitch):
        offs[p] = running
        running = running + counts[p]
    first = offs[pitch_next] // KB
    loads["fields"].wait()

    for f in range(nf):
        for r in range(0, rows, 8):
            for q in range(cols // 128):
                at = pl.ds((r * (cols // 128) + q) * 8 + f, 8, stride=cols // 16)
                table[at, :] = fields[f, r : r + 8, q * 128 : (q + 1) * 128]
    for f in range(nf):
        for q in range(chunks):
            x = fields[f, :, q * B : (q + 1) * B]
            hi = x.astype(BF)
            at = f * A + q * rows
            pair[at : at + rows, 0:B] = hi
            pair[at : at + rows, B : 2 * B] = (x - hi.astype(F32)).astype(BF)
    tiles = table.reshape(rows * cols // 128, 8, 128)

    lane = lax.broadcasted_iota(jnp.int32, (rows, 128), 1)
    mean = jnp.zeros((rows, 128), F32)
    left = jnp.zeros((rows, 128), F32)
    right = jnp.zeros((rows, 128), F32)
    for f in range(nf):
        x = fields[f]
        mean = jnp.where(lane == f, jnp.sum(x, axis=1, keepdims=True) * (1.0 / cols), mean)
        left = jnp.where(lane == f, x[:, 0:1], left)
        right = jnp.where(lane == f, x[:, cols - 1 : cols], right)
        row_out[0, f : f + 1, :] = x[0:1, :]
        row_out[1, f : f + 1, :] = x[rows - 1 : rows, :]
    col_out[0] = left
    col_out[1] = right
    mine = pl.ds(pl.multiple_of(sp * rows, rows), rows)
    profile[mine, :] = mean

    diag = lax.broadcasted_iota(jnp.int32, (nq, nq), 0) == lax.broadcasted_iota(
        jnp.int32, (nq, nq), 1
    )

    def column(line):
        return jnp.sum(jnp.where(diag, line, 0.0), axis=1, keepdims=True)

    for name in ("relax", "drag", "couple"):
        loads[name].wait()
    keep = column(1.0 - relax[...])
    pull = [column(drag[f : f + 1, :]) for f in range(nf)]
    cp = couple[...]
    index_a = lax.broadcasted_iota(jnp.int32, (A, KB), 0)
    index_b = lax.broadcasted_iota(jnp.int32, (B, KB), 0)
    lane_8 = lax.broadcasted_iota(jnp.int32, (8, 128), 1)
    lane_q = lax.broadcasted_iota(jnp.int32, (nq, 128), 1)

    def block_of(s):
        return lax.rem(first + s, blocks)

    def cells_of(block, low):
        homes = cell[block]
        c = jnp.concatenate([homes[q : q + 1] for q in range(low, KB // 128)], axis=1)
        in_row = c & (cols - 1)
        hot_a = index_a[:, low * 128 :] == (in_row // B) * rows + c // cols
        hot_b = jnp.where(index_b[:, low * 128 :] == (in_row & (B - 1)), 1.0, 0.0).astype(BF)
        return hot_a, hot_b

    def gather_by_matmul(s, low):
        block = block_of(s)
        hot_a, hot_b = cells_of(block, low)
        picked = jnp.dot(
            pair[...], jnp.concatenate([hot_b, hot_b], axis=0), preferred_element_type=F32
        )
        value = keep * records[block, :, low * 128 :]
        for f in range(nf):
            fluid = jnp.sum(
                jnp.where(hot_a, picked[f * A : (f + 1) * A], 0.0), axis=0, keepdims=True
            )
            value = value + pull[f] * fluid
        for q in range(low, KB // 128):
            moved[s * (KB // 128) + q] = value[:, (q - low) * 128 : (q - low + 1) * 128]

    def gather(s, high):
        block = block_of(s)
        for h in range(high):
            row = block * (KB // 128) + h
            fluid = jnp.zeros((8, 128), F32)
            for j in range(128):
                found = pltpu.roll(tiles[place_s[0, row, j]], place_s[1, row, j], axis=1)
                fluid = jnp.where(lane_8 == j, found, fluid)
            value = keep * records[block, :, h * 128 : (h + 1) * 128]
            for f in range(nf):
                value = value + pull[f] * fluid[f : f + 1, :]
            moved[s * (KB // 128) + h] = value

    def pack(k, slot):
        p = lax.rem(me + k, n_pitch)
        count = counts[p]
        start = lax.rem(offs[p] - first * KB + npar, npar)
        tile = start // 128
        pieces = [moved[tile + q] for q in range(cap // 128 + 1)]
        shift = lax.rem(start, 128)
        turned = [pltpu.roll(piece, lax.rem(128 - shift, 128), axis=1) for piece in pieces]
        for q in range(cap // 128):
            piece = jnp.where(lane_q < 128 - shift, turned[q], turned[q + 1])
            outgoing[slot, :, q * 128 : (q + 1) * 128] = jnp.where(
                lane_q + q * 128 < count, piece, 0.0
            )

    own_slots = pl.ds(pl.multiple_of(me * cap, cap), cap)

    def parcel_copy(k):
        return pltpu.make_async_remote_copy(
            src_ref=outgoing.at[k],
            dst_ref=arrived.at[:, own_slots],
            send_sem=send_sem.at[k],
            recv_sem=recv_sem.at[k],
            device_id=(lax.rem(me + k, n_pitch), sp),
            device_id_type=MESH,
        )

    def profile_copy(k):
        return pltpu.make_async_remote_copy(
            src_ref=profile.at[mine],
            dst_ref=profile.at[mine],
            send_sem=prof_send.at[k],
            recv_sem=prof_recv.at[k],
            device_id=(me, lax.rem(sp + k, n_span)),
            device_id_type=MESH,
        )

    def halo_copies(turn):
        copies = []
        for side in range(2):
            for kind, (out, into, target) in enumerate(
                (
                    (row_out, row_in, (me, (span_prev, span_next)[side])),
                    (col_out, col_in, ((pitch_prev, pitch_next)[side], sp)),
                )
            ):
                copies.append(
                    pltpu.make_async_remote_copy(
                        src_ref=out.at[2 * turn + side],
                        dst_ref=into.at[2 * turn + side],
                        send_sem=halo_send.at[4 * turn + 2 * side + kind],
                        recv_sem=halo_recv.at[4 * turn + 2 * side + kind],
                        device_id=target,
                        device_id_type=MESH,
                    )
                )
        return copies

    for load in record_loads:
        load.wait()
    place_copy.wait()
    total[...] = jnp.zeros_like(total)

    def start_profile(k, _):
        profile_copy(k).start()
        return 0

    first_halo = halo_copies(0)

    def scatter(steps):
        left_side, right_side = [], []
        for s in steps:
            block = block_of(s)
            hot_a, hot_b = cells_of(block, 0)
            par = records[block]
            given = jnp.zeros((nf, KB), F32)
            for q in range(nq):
                given = given + cp[:, q : q + 1] * par[q : q + 1, :]
            hi = given.astype(BF).astype(F32)
            lo = given - hi
            for x in (hi, lo):
                left_side.append(
                    jnp.concatenate(
                        [jnp.where(hot_a, x[f : f + 1], 0.0).astype(BF) for f in range(nf)],
                        axis=0,
                    )
                )
                right_side.append(hot_b)
        total[...] += lax.dot_general(
            jnp.concatenate(left_side, axis=1),
            jnp.concatenate(right_side, axis=1),
            (((1,), (1,)), ((), ())),
            preferred_element_type=F32,
        )

    def wait_profile(k, _):
        profile_copy(k).wait()
        return 0

    def rate_of(part, parts):
        at = pl.ds(pl.multiple_of(part * (cols // parts), cols // parts), cols // parts)
        x = fields[0, :, at] + corr[:, 0:1]
        rate[:, at] = (jnp.maximum(x, 0.0) + jnp.log1p(jnp.exp(-jnp.abs(x)))) * (
            1.0 + jnp.tanh(fields[1, :, at] + corr[:, 1:2])
        )

    def gather_only(s, _):
        gather(s, KB // 256)
        gather_by_matmul(s, KB // 256)
        pack(s, s)

        @pl.when(s == 0)
        def _():
            pl.semaphore_wait(barrier, n_pitch + n_span - 2)
            lax.fori_loop(1, n_span, start_profile, 0)
            for copy in first_halo:
                copy.start()

        @pl.when(s >= 1)
        def _():
            parcel_copy(s).start()

        return 0

    lax.fori_loop(0, ALONE, gather_only, 0)
    for name in ("mixing", "nu", "gain", "advection"):
        loads[name].wait()
    lax.fori_loop(1, n_span, wait_profile, 0)
    corr[...] = jnp.dot(
        mixing[mine, :], profile[...], precision=lax.Precision.HIGHEST, preferred_element_type=F32
    )

    def gather_and_scatter(s, _):
        gather(s, KB // 128)
        scatter([s])
        pack(s, s)
        parcel_copy(s).start()
        rate_of(s - ALONE, blocks - ALONE)
        return 0

    lax.fori_loop(ALONE, blocks, gather_and_scatter, 0)
    for q in range(KB // 128):
        moved[npar // 128 + q] = moved[q]

    def send(k, _):
        pack(k, k)
        parcel_copy(k).start()
        return 0

    lax.fori_loop(blocks, blocks + AHEAD, send, 0)

    def scatter_rest(t, _):
        scatter([2 * t, 2 * t + 1])
        for n in range(EACH):
            send(blocks + AHEAD + EACH * t + n, 0)
        return 0

    lax.fori_loop(0, ALONE // 2, scatter_rest, 0)

    for f in range(nf):
        deposit = jnp.concatenate(
            [total[f * A + q * rows : f * A + (q + 1) * rows, :] for q in range(chunks)], axis=1
        )
        source[f] = 0.25 * (cond_gain[f] * rate[...] - 0.5 * corr[:, f : f + 1] + deposit)

    row_id = lax.broadcasted_iota(jnp.int32, (rows, cols), 0)
    col_id = lax.broadcasted_iota(jnp.int32, (rows, cols), 1)
    row_low = jnp.where(sp == 0, 0.0, 1.0)
    row_high = jnp.where(sp == n_span - 1, 0.0, 1.0)
    col_low = jnp.where(me == 0, 0.0, 1.0)
    col_high = jnp.where(me == n_pitch - 1, 0.0, 1.0)

    def advance(u, f, turn):
        below = row_in[2 * turn + 1, f : f + 1, :] * row_low
        above = row_in[2 * turn, f : f + 1, :] * row_high
        before = col_in[2 * turn + 1][:, f : f + 1] * col_low
        after = col_in[2 * turn][:, f : f + 1] * col_high
        upper = jnp.where(row_id == rows - 1, above, pltpu.roll(u, rows - 1, axis=0))
        lower = jnp.where(row_id == 0, below, pltpu.roll(u, 1, axis=0))
        ahead = jnp.where(col_id == cols - 1, after, pltpu.roll(u, cols - 1, axis=1))
        behind = jnp.where(col_id == 0, before, pltpu.roll(u, 1, axis=1))
        return (
            u
            + source[f]
            + advection[0, f] * (upper - lower)
            + advection[1, f] * (ahead - behind)
            + nu[...] * (upper + lower + ahead + behind - 4.0 * u)
        )

    for copy in first_halo:
        copy.wait()
    left = jnp.zeros((rows, 128), F32)
    right = jnp.zeros((rows, 128), F32)
    for f in range(nf):
        u = advance(fields[f], f, 0)
        state[f] = u
        left = jnp.where(lane == f, u[:, 0:1], left)
        right = jnp.where(lane == f, u[:, cols - 1 : cols], right)
        row_out[2, f : f + 1, :] = u[0:1, :]
        row_out[3, f : f + 1, :] = u[rows - 1 : rows, :]
    col_out[2] = left
    col_out[3] = right
    second_halo = halo_copies(1)
    for copy in second_halo:
        copy.start()
    lax.fori_loop(blocks + AHEAD + EACH * (ALONE // 2), n_pitch, send, 0)
    pack(n_pitch, 0)
    own_copy = pltpu.make_async_copy(outgoing.at[0], arrived.at[:, own_slots], own_sem)
    own_copy.start()

    for copy in second_halo:
        copy.wait()
    for f in range(nf):
        fields[f] = advance(state[f], f, 1)
        pltpu.make_async_copy(fields.at[f], new_fields.at[f], out_sem.at[f]).start()
    for f in range(nf):
        pltpu.make_async_copy(fields.at[f], new_fields.at[f], out_sem.at[f]).wait()

    own_copy.wait()

    def wait_parcels(k, _):
        parcel_copy(k).wait()
        return 0

    lax.fori_loop(1, n_pitch, wait_parcels, 0)


def hand_over_kernel(fields_from, arrived_from, fields_to, arrived_to, held, slots, sem_a, sem_b):
    parts = sem_b.shape[1]
    width = slots.shape[1] // parts
    ways = [
        (fields_from.at[f], held.at[f], fields_to.at[f], sem_a.at[0, f], sem_a.at[1, f])
        for f in range(held.shape[0])
    ]
    for q in range(parts):
        at = slice(q * width, (q + 1) * width)
        ways.append(
            (
                arrived_from.at[:, at],
                slots.at[:, at],
                arrived_to.at[:, at],
                sem_b.at[0, q],
                sem_b.at[1, q],
            )
        )
    into = [pltpu.make_async_copy(a, b, s) for a, b, _, s, _ in ways]
    out = [pltpu.make_async_copy(b, c, s) for _, b, c, _, s in ways]
    for copy in into:
        copy.start()
    for first, second in zip(into, out):
        first.wait()
        second.start()
    for copy in out:
        copy.wait()


def local(
    fields, diffusivity, mixing, cond_gain, advection, parcels, cell, couple, relax, drag, counts
):
    nf, rows, cols = fields.shape
    nq, npar = parcels.shape
    n_pitch, n_span = lax.axis_size("pitch"), lax.axis_size("span")
    cap = 2 * npar // n_pitch
    hbm = pl.BlockSpec(memory_space=pl.ANY)
    dma = pltpu.SemaphoreType.DMA
    results = pl.pallas_call(
        functools.partial(step_kernel, n_pitch, n_span, cap),
        out_shape=(
            jax.ShapeDtypeStruct(fields.shape, F32),
            jax.ShapeDtypeStruct((nq, n_pitch * cap), F32),
        ),
        in_specs=[hbm] * 11,
        out_specs=(hbm, hbm),
        scratch_shapes=[
            pltpu.SMEM((n_pitch,), jnp.int32),
            pltpu.SMEM((nf,), F32),
            pltpu.SMEM((2, nf), F32),
            pltpu.VMEM((npar // KB, KB // 128, 128), jnp.int32),
            pltpu.VMEM(fields.shape, F32),
            pltpu.VMEM((rows, cols), F32),
            pltpu.VMEM(mixing.shape, F32),
            pltpu.VMEM((nf, nq), F32),
            pltpu.VMEM((1, nq), F32),
            pltpu.VMEM((nf, nq), F32),
            dma((10,)),
            dma((npar // KB,)),
            pltpu.SMEM((n_pitch,), jnp.int32),
            pltpu.VMEM((rows * cols // 16, 128), F32),
            pltpu.VMEM((nf * A, 2 * B), BF),
            pltpu.VMEM((rows, 128), F32),
            pltpu.VMEM((rows, cols), F32),
            pltpu.VMEM((2, npar // 128, 128), jnp.int32),
            pltpu.SMEM((2, npar // 128, 128), jnp.int32),
            dma,
            pltpu.VMEM((nf * A, B), F32),
            pltpu.VMEM(((npar + KB) // 128, nq, 128), F32),
            pltpu.VMEM((npar // KB, nq, KB), F32),
            pltpu.VMEM((n_pitch, nq, cap), F32),
            pltpu.VMEM((n_span * rows, 128), F32),
            pltpu.VMEM(fields.shape, F32),
            pltpu.VMEM(fields.shape, F32),
            pltpu.VMEM((4, 8, cols), F32),
            pltpu.VMEM((4, 8, cols), F32),
            pltpu.VMEM((4, rows, 128), F32),
            pltpu.VMEM((4, rows, 128), F32),
            dma((n_pitch,)),
            dma((n_pitch,)),
            dma((n_span,)),
            dma((n_span,)),
            dma((8,)),
            dma((8,)),
            dma,
            dma((nf,)),
        ],
        compiler_params=pltpu.CompilerParams(
            collective_id=0, has_side_effects=True, vmem_limit_bytes=60 << 20
        ),
        cost_estimate=pl.CostEstimate(
            flops=8 * nf * rows * cols * npar, bytes_accessed=6 << 20, transcendentals=0
        ),
    )(
        counts,
        cond_gain,
        advection.T,
        cell.reshape(npar // KB, KB // 128, 128),
        fields,
        diffusivity,
        mixing,
        parcels,
        couple,
        relax.reshape(1, nq),
        drag.T,
    )
    return pl.pallas_call(
        hand_over_kernel,
        out_shape=tuple(jax.ShapeDtypeStruct(x.shape, x.dtype) for x in results),
        in_specs=[hbm] * 2,
        out_specs=(hbm, hbm),
        scratch_shapes=[
            pltpu.VMEM(results[0].shape, F32),
            pltpu.VMEM(results[1].shape, F32),
            dma((2, nf)),
            dma((2, 4)),
        ],
        compiler_params=pltpu.CompilerParams(vmem_limit_bytes=60 << 20),
    )(*results)


def solution(mesh):
    return jax.shard_map(
        local,
        mesh=mesh,
        in_specs=(
            P(None, "span", "pitch"),
            P("span", "pitch"),
            P(),
            P(),
            P(),
            P(None, ("pitch", "span")),
            P(("pitch", "span")),
            P(),
            P(),
            P(),
            P(("pitch", "span")),
        ),
        out_specs=(P(None, "span", "pitch"), P(None, ("pitch", "span"))),
        check_vma=False,
    )
```
